128 devices in a mesh: row: 8 (over z, x_hi), col: 16 (over y, x_lo, core).
Axes of the slice: x: 4 (x_hi: 2, x_lo: 2; x = x_hi * 2 + x_lo), y: 4, z: 4, core: 2. Of those that a mesh axis runs over, the one named last changes fastest.
Arguments:
- factor: bfloat16 [16384, 16384], P('row', 'col'), may hold values from -1 to 7, as said below
- old_basis: bfloat16 [16384, 2048], P(('col', 'row')), may hold values from -9 to 9, as said below
- first_moment: float32 [16384, 2048], P(('col', 'row')), may hold values from -1.8 to 1.8
Outputs:
- new_basis: bfloat16 [16384, 2048], P(('col', 'row'))
- rotated_moment: float32 [16384, 2048], P(('col', 'row'))
The draws below stay inside these ranges and needn't reach their ends.
Inputs may be any that keep to these rules, and one draw needn't show every extreme that they name: factor equals its transpose and is positive definite. old_basis has full column rank.
All inputs are finite; a program needn't handle non-finite values.
Results may differ from the reference program's by a relative error of at most 0.0053.
Values may be sent and summed in bfloat16 or wider, within the bound.
A program may use at most 192 MiB of HBM per device.

```python
import math
import jax
import jax.numpy as jnp
from jax import lax

M = 16384
K = 2048


def draw_factor(key, part):
    key = jax.random.fold_in(key, 11)
    noise_key, diag_key = jax.random.split(key)
    noise = jnp.clip(jax.random.normal(noise_key, (M, M), jnp.float32), -5.0, 5.0)
    spread = (noise + noise.T) * (0.6 / math.sqrt(2.0 * M))
    diagonal = jnp.exp(jax.random.uniform(diag_key, (M,), jnp.float32, math.log(2.0), math.log(6.0)))
    places = jnp.arange(M)
    spread = spread.at[places, places].add(diagonal)
    return spread.astype(jnp.bfloat16)


def draw_old_basis(key, part):
    key = jax.random.fold_in(key, 23)
    values = jnp.clip(jax.random.normal(key, (M, K), jnp.float32), -4.5, 4.5)
    ramp = 0.6 + 1.2 * (jnp.arange(M, dtype=jnp.float32) + 0.5) / M
    return (values * ramp[:, None]).astype(jnp.bfloat16)


def block_levels(key, extent, cuts, least, high):
    level = 1.0
    for axis_at, shards_of in cuts:
        heights = jax.random.uniform(jax.random.fold_in(jax.random.fold_in(key, 6), axis_at), (shards_of,), jnp.float32, least / len(cuts), high / len(cuts))
        level = level * jnp.repeat(jnp.exp(heights), extent[axis_at] // shards_of).reshape((-1,) + (1,) * (len(extent) - 1 - axis_at))
    return level


def centred(stream_key, extent, deviation, most, cuts=(), kind=jnp.bfloat16):
    loudness = block_levels(stream_key, extent, cuts, -0.22, 0.18) if cuts else 1.0
    values = jax.random.normal(stream_key, extent, jnp.float32) * deviation * loudness
    return jnp.minimum(jnp.maximum(values, -most), most).astype(kind)


def setup_inputs(seed: int = 0) -> dict:
    arg_keys = jax.random.split(jax.random.key(seed), 4)
    factor = draw_factor(jax.random.fold_in(arg_keys[3], 71), 0)
    old_basis = draw_old_basis(jax.random.fold_in(arg_keys[3], 71), 0)
    first_moment = centred(arg_keys[2], (M, K), 0.3, 1.8, ((0, 128),), jnp.float32)
    return dict(factor=factor, old_basis=old_basis, first_moment=first_moment)


def reference(factor, old_basis, first_moment):
    block_rows = M // 8
    blocks = factor.reshape(8, block_rows, M)

    def one_block(row_block):
        return jnp.dot(row_block.astype(jnp.float32), old_basis.astype(jnp.float32), preferred_element_type=jnp.float32).astype(jnp.bfloat16)
    product = lax.map(one_block, blocks).reshape(M, K)
    gram_matrix = lax.dot_general(product.astype(jnp.float32), product.astype(jnp.float32), (((0,), (0,)), ((), ())), preferred_element_type=jnp.float32)
    gram_matrix = gram_matrix * (1.0 / M)
    lower_factor = jnp.linalg.cholesky(gram_matrix)
    solved = jax.scipy.linalg.solve_triangular(lower_factor, product.astype(jnp.float32).T, lower=True)
    new_basis = solved.T.astype(jnp.bfloat16)
    rotated_moment = jnp.dot(first_moment, lower_factor, precision=lax.Precision.HIGHEST)
    return (new_basis, rotated_moment)
```

```python
import jax
import jax.numpy as jnp
from jax import lax
from jax.experimental import pallas as pl
from jax.experimental.pallas import tpu as pltpu
from jax.sharding import PartitionSpec as P

M = 16384
F32, BF = jnp.float32, jnp.bfloat16


def split(x):
    hi = x.astype(BF)
    return hi, (x - hi.astype(F32)).astype(BF)


def factor_block(d_ref, w_ref, width=16):
    n = 128
    rows_i = lax.broadcasted_iota(jnp.int32, (n, n), 0)
    cols_i = lax.broadcasted_iota(jnp.int32, (n, n), 1)
    w_ref[...] = jnp.where(rows_i == cols_i, 1.0, 0.0).astype(F32)
    np_ = n // width
    R, V = d_ref[:width, :], w_ref[:width, :]
    for p in range(np_):
        b0, m0, m1 = width * p, width * (p + 1), width * (p + 2)
        more = p < np_ - 1
        if more:
            N, NV = d_ref[m0:m1, :], w_ref[m0:m1, :]
            A = jnp.concatenate([R, N], 0)
            Z = jnp.concatenate([V, NV], 0)
        else:
            A, Z = R, V
        H = A.shape[0]
        C = [jnp.broadcast_to(A[:, b0 + b:b0 + b + 1], (H, n)) for b in range(width)]
        us, vs = [], []
        def sub(x, a):
            return x[a:a + 1, :]
        lo = 0
        for a in range(width):
            if a - lo == 8:
                C = [None if c is None else c[8:] for c in C]
                A, Z = A[8:], Z[8:]
                lo = a
            q = a - lo
            r = lax.rsqrt(sub(C[a], q))
            u, v = sub(A, q) * r, sub(Z, q) * r
            us.append(u); vs.append(v)
            ca = C[a] * r
            C[a] = None
            for b in range(a + 1, width):
                C[b] = C[b] - ca * jnp.broadcast_to(sub(ca, b - lo), ca.shape)
            A = A - ca * u
            Z = Z - ca * v
        U, W = jnp.concatenate(us, 0), jnp.concatenate(vs, 0)
        d_ref[b0:m0, :] = U
        w_ref[b0:m0, :] = W
        if more:
            R, V = A[width - lo:], Z[width - lo:]
        if p < np_ - 2:
            uh, ul = split(U)
            wh, wl = split(W)
            lhs = jnp.concatenate([uh, ul, uh], 0)
            rhs = jnp.concatenate([jnp.concatenate([uh, uh, ul], 0), jnp.concatenate([wh, wh, wl], 0)], 1)
            up = lax.dot_general(lhs, rhs, (((0,), (0,)), ((), ())), preferred_element_type=F32)
            d_ref[m1:, :] = d_ref[m1:, :] - up[m1:, :n]
            w_ref[m1:, :] = w_ref[m1:, :] - up[m1:, n:]
    d_ref[...] = jnp.where(rows_i <= cols_i, d_ref[...], 0.0)


B = 256
NT=(((1,),(1,)),((),()))
NN=(((1,),(0,)),((),()))
def mm(a,b,dims): return lax.dot_general(a,b,dims,preferred_element_type=F32)
def mm3(ah,al,bh,bl,dims): return mm(ah,bh,dims)+(mm(ah,bl,dims)+mm(al,bh,dims))
def mm3f(a,b,dims):
    ah,al=split(a); bh,bl=split(b)
    return mm3(ah,al,bh,bl,dims)

def factor_solve_kernel(g_ref, p_ref, m_ref, x_ref, y_ref, A, Lh, Ll, mh, ml, d_s, w_s, w_full, gsem):
    n = g_ref.shape[0]
    nb = n // B
    copies = [pltpu.make_async_copy(g_ref.at[pl.ds(k*B, n-k*B), pl.ds(k*B, B)], A.at[pl.ds(k*B, n-k*B), pl.ds(k*B, B)], gsem.at[k]) for k in range(nb)]
    for c in copies: c.start()
    A[n:n+128, :] = p_ref[...].astype(F32)
    A[n+128:, :] = jnp.zeros((128, n), F32)
    mhi, mlo = split(m_ref[...])
    mh[...] = mhi; ml[...] = mlo
    def blk(i, k): return (pl.ds(pl.multiple_of(i*B, B), B), pl.ds(pl.multiple_of(k*B, B), B))
    for c in copies: c.wait()
    def step(k, carry):
        def row_tile(i, _):
            t = blk(i, k)
            def inner(j, acc):
                a, b = blk(i, j), blk(k, j)
                return acc - mm3(Lh[a], Ll[a], Lh[b], Ll[b], NT)
            A[t] = lax.fori_loop(0, k, inner, A[t])
            return 0
        lax.fori_loop(k, nb+1, row_tile, 0)
        kk = pl.multiple_of(k*B, B)
        h = 128
        q0, q1 = pl.ds(kk, h), pl.ds(kk+h, h)
        d_s[...] = A[q0, q0]
        factor_block(d_s, w_s)
        w0 = w_s[...]
        l00 = d_s[...].T
        l10 = mm3f(A[q1, q0], w0, NT)
        d_s[...] = A[q1, q1] - mm3f(l10, l10, NT)
        factor_block(d_s, w_s)
        w1 = w_s[...]
        l11 = d_s[...].T
        w10 = -mm3f(w1, mm3f(l10, w0, NN), NN)
        w_full[:h, :h] = w0
        w_full[:h, h:] = jnp.zeros((h, h), F32)
        w_full[h:, :h] = w10
        w_full[h:, h:] = w1
        for (r, c, v) in ((q0,q0,l00),(q0,q1,jnp.zeros((h,h),F32)),(q1,q0,l10),(q1,q1,l11)):
            hi, lo = split(v)
            Lh[r,c]=hi; Ll[r,c]=lo
        wh, wl = split(w_full[...])
        def panel(i, _):
            t = blk(i, k)
            ah, al = split(A[t])
            v = mm3(ah, al, wh, wl, NT)
            hi, lo = split(v)
            Lh[t] = hi; Ll[t] = lo
            return 0
        lax.fori_loop(k+1, nb+1, panel, 0)
        x_ref[:, pl.ds(kk, B)] = (Lh[n:n+128, pl.ds(kk, B)].astype(F32)+Ll[n:n+128, pl.ds(kk, B)].astype(F32)).astype(BF)
        def yt(i, acc):
            a = pl.ds(pl.multiple_of(i*B,B),B)
            t = blk(i, k)
            return acc + mm3(mh[:, a], ml[:, a], Lh[t], Ll[t], NN)
        y_ref[:, pl.ds(kk, B)] = lax.fori_loop(k, nb, yt, jnp.zeros((128, B), F32))
        return carry
    lax.fori_loop(0, nb, step, 0)

def factor_solve(g, p, m):
    n=g.shape[0]
    return pl.pallas_call(factor_solve_kernel,
        out_shape=[jax.ShapeDtypeStruct((128,n),BF), jax.ShapeDtypeStruct((128,n),F32)],
        in_specs=[pl.BlockSpec(memory_space=pl.ANY), pl.BlockSpec(memory_space=pltpu.VMEM), pl.BlockSpec(memory_space=pltpu.VMEM)],
        out_specs=[pl.BlockSpec(memory_space=pltpu.VMEM)]*2,
        scratch_shapes=[pltpu.VMEM((n+B,n),F32),pltpu.VMEM((n+B,n),BF),pltpu.VMEM((n+B,n),BF),pltpu.VMEM((128,n),BF),pltpu.VMEM((128,n),BF),
          pltpu.VMEM((128,128),F32),pltpu.VMEM((128,128),F32),pltpu.VMEM((B,B),F32),pltpu.SemaphoreType.DMA((n//B,))],
        compiler_params=pltpu.CompilerParams(vmem_limit_bytes=60*2**20),
        name="factor_solve")(g,p,m)


def body(factor, old_basis, first_moment):
    grid_rows = lax.axis_size("row")
    grid_columns = lax.axis_size("col")
    tile_rows, tile_columns = factor.shape
    slab_rows, panel_width = old_basis.shape
    groups = grid_columns // grid_rows
    column_panel = lax.all_gather(old_basis, "row", axis=0, tiled=True)
    sub_rows = slab_rows // grid_columns
    arranged = factor.reshape(groups, grid_rows, grid_columns, sub_rows, tile_columns)
    stripe = arranged
    stripe = jnp.transpose(stripe, (2, 1, 0, 3, 4)).reshape(
        lax.axis_size("col") * slab_rows, tile_columns
    )
    summed = lax.psum_scatter(
        jnp.dot(stripe, column_panel, preferred_element_type=jnp.float32),
        "col",
        scatter_dimension=0,
        tiled=True,
    )
    relayed = summed.astype(jnp.bfloat16).reshape(grid_rows, groups, sub_rows, panel_width)
    relayed = lax.all_to_all(relayed, "row", split_axis=0, concat_axis=0, tiled=True)
    relayed = relayed.reshape(grid_columns, sub_rows, panel_width)
    relayed = lax.all_to_all(relayed, "col", split_axis=0, concat_axis=0, tiled=True)
    product = relayed.reshape(slab_rows, panel_width)
    gram_part = lax.dot_general(
        product, product, (((0,), (0,)), ((), ())), preferred_element_type=jnp.float32
    )
    gram_part = gram_part * (1.0 / M)
    gram_matrix = lax.psum(gram_part, ("row", "col"))
    new_basis, rotated_moment = factor_solve(gram_matrix, product, first_moment)
    return (new_basis, rotated_moment)


def solution(mesh):
    placed = (P("row", "col"), P(("col", "row"), None), P(("col", "row"), None))
    return jax.shard_map(
        body,
        mesh=mesh,
        in_specs=placed,
        out_specs=(P(("col", "row"), None), P(("col", "row"), None)),
        check_vma=False,
    )
```

```python
import functools

import jax
import jax.numpy as jnp
from jax import lax
from jax.experimental import pallas as pl
from jax.experimental.pallas import tpu as pltpu
from jax.sharding import PartitionSpec as P

M = 16384
F32, BF = jnp.float32, jnp.bfloat16
MESH = pl.DeviceIdType.MESH
TN = (((0,), (0,)), ((), ()))

def coords():
    row, col = lax.axis_index("row"), lax.axis_index("col")
    return (row % 2) * 2 + (col // 2) % 2, col // 4, row // 2, col % 2

def device(x, y, z, core):
    return (z * 2 + x // 2, y * 4 + (x % 2) * 2 + core)

def links(x, y, z, core):
    near = lambda v: v + 1 - 2 * (v % 2)
    far = lambda v: 3 - v
    low = lambda v: (v + v // 2) % 2
    peers = [device(near(x), y, z, core), device(x, near(y), z, core), device(x, y, near(z), core),
             device(far(x), y, z, core), device(x, far(y), z, core), device(x, y, far(z), core)]
    bits = [low(x), low(y), low(z), x // 2, y // 2, z // 2]
    return peers, bits

def strips(n):
    lens = [n // 256 - c // 2 for c in range(n // 128)]
    starts = [sum(lens[:c]) for c in range(len(lens) + 1)]
    return lens, starts

def remote(src, dst, ssem, rsem, dev):
    return pltpu.make_async_remote_copy(src, dst, ssem, rsem, device_id=dev, device_id_type=MESH)

def gram_kernel(p_ref, g_ref, own_ref, W, RB, O, ss, rs, as_, ar, fs, fr, ls, ps, pr):
    x, y, z, core = coords()
    row, col = lax.axis_index("row"), lax.axis_index("col")
    peers, bits = links(x, y, z, core)
    sib = device(x, y, z, 1 - core)
    n = p_ref.shape[1]
    lens, starts = strips(n)
    parts, rows = W.shape[0], W.shape[1]
    tiles = rows // 256
    j = 2 * (col // 2) + 1 - core
    to = (j % 8, 2 * row + j // 8)
    i = (col % 2) * 8 + row
    frm = (col // 2, (i // 2) * 2 + 1 - i % 2)
    bar = pltpu.get_barrier_semaphore()
    for d in peers + [sib, frm]:
        pl.semaphore_signal(bar, inc=1, device_id=d, device_id_type=MESH)
    pl.semaphore_wait(bar, 8)

    def tile(s, u, _):
        U = core * (parts * tiles) + s * tiles + u
        c, st = 0, 0
        for q in range(1, len(lens)):
            past = (U >= starts[q]).astype(jnp.int32)
            c, st = c + past, st + past * lens[q - 1]
        i = U - st + c // 2
        a = p_ref[:, pl.ds(pl.multiple_of(i * 256, 256), 256)]
        b = p_ref[:, pl.ds(pl.multiple_of(c * 128, 128), 128)]
        W[s, pl.ds(pl.multiple_of(u * 256, 256), 256), :] = lax.dot_general(a, b, TN, preferred_element_type=F32) * (1.0 / M)
        return 0

    slab = remote(p_ref.at[pl.ds(pl.multiple_of((1 - core) * 128, 128), 128), :], own_ref, ps, pr, to)
    slab.start()

    off = [0] * parts
    steps = len(peers)
    sends = []
    def send(t, s):
        h = rows >> (t + 1)
        d = (s + t) % steps
        src = W.at[s, pl.ds(pl.multiple_of(off[s] + (1 - bits[d]) * h, 8), h), :]
        c = remote(src, RB.at[s, pl.ds(rows - 2 * h, h), :], ss.at[t, s], rs.at[t, s], peers[d])
        c.start()
        return c
    cur = []
    for s in range(parts):
        lax.fori_loop(0, tiles, functools.partial(tile, s), 0)
        cur.append(send(0, s))
    for t in range(steps):
        h = rows >> (t + 1)
        nxt = []
        for s in range(parts):
            cur[s].wait_recv()
            d = (s + t) % steps
            off[s] = off[s] + bits[d] * h
            at = pl.ds(pl.multiple_of(off[s], 8), h)
            if t < steps - 1:
                W[s, at, :] = W[s, at, :] + RB[s, pl.ds(rows - 2 * h, h), :]
                sends.append(cur[s])
                nxt.append(send(t + 1, s))
            else:
                O[s, at, :] = W[s, at, :] + RB[s, pl.ds(rows - 2 * h, h), :]
                sends.append(cur[s])
        cur = nxt
    tail = []
    def share(s, at, q):
        c = remote(O.at[s, at, :], g_ref.at[core, s, at, :], fs.at[q, s], fr.at[q, s], sib)
        l = pltpu.make_async_copy(O.at[s, at, :], g_ref.at[core, s, at, :], ls.at[q, s])
        c.start(); l.start()
        tail.append((c, l))
    def give(t, s):
        h = rows >> (t + 1)
        at = pl.ds(pl.multiple_of(off[s], 8), h)
        c = remote(O.at[s, at, :], O.at[s, at, :], as_.at[t, s], ar.at[t, s], peers[(s + t) % steps])
        c.start()
        return c
    cur = [give(steps - 1, s) for s in range(parts)]
    for t in range(steps - 1, -1, -1):
        h = rows >> (t + 1)
        nxt = []
        for s in range(parts):
            cur[s].wait_recv()
            b = bits[(s + t) % steps]
            got = off[s] + (1 - 2 * b) * h
            off[s] = off[s] - b * h
            sends.append(cur[s])
            if t > 0:
                nxt.append(give(t - 1, s))
            if t == 2:
                share(s, pl.ds(pl.multiple_of(off[s], 8), 2 * h), 2)
            elif t < 2:
                share(s, pl.ds(pl.multiple_of(got, 8), h), t)
        cur = nxt
    for c in sends:
        c.wait_send()
    for c, l in tail:
        l.wait()
        c.wait()
    slab.wait()

def gram_sum(p2):
    n = p2.shape[1]
    lens, starts = strips(n)
    rows = starts[-1] * 256 // 12
    dma = pltpu.SemaphoreType.DMA
    return pl.pallas_call(
        gram_kernel,
        out_shape=[jax.ShapeDtypeStruct((2, 6, rows, 128), F32), jax.ShapeDtypeStruct((128, n), BF)],
        in_specs=[pl.BlockSpec(memory_space=pltpu.VMEM)],
        out_specs=[pl.BlockSpec(memory_space=pl.ANY)] * 2,
        scratch_shapes=[pltpu.VMEM((6, rows, 128), F32)] * 3 + [dma((6, 6))] * 4 + [dma((3, 6))] * 3 + [dma(())] * 2,
        compiler_params=pltpu.CompilerParams(collective_id=1, has_side_effects=True, vmem_limit_bytes=40 * 2**20),
        name="gram_sum",
    )(p2)


NN = (((1,), (0,)), ((), ()))

def product_kernel(f_ref, q_ref, p_ref, F, Q, S, own, YR, XS, XR, P2, fsem, qs, qr, gs, gr, ys, yr, xs, xr, ps, pr):
    x, y, z, core = coords()
    row, col = lax.axis_index("row"), lax.axis_index("col")
    chunks, wide = Q.shape[0], Q.shape[3]
    half = chunks * wide
    sib = device(x, y, z, 1 - core)
    across = device((x + 2) % 4, y, z, core)
    beside = device(x + 1 - 2 * (x % 2), y, z, core)
    zs = [device(x, y, (z + k) % 4, core) for k in (1, 2, 3)]
    yy = [device(x, (y + k) % 4, z, core) for k in (1, 2, 3)]
    bar = pltpu.get_barrier_semaphore()
    for d in [sib, across, beside] + zs + yy:
        pl.semaphore_signal(bar, inc=1, device_id=d, device_id_type=MESH)
    pl.semaphore_wait(bar, 9)
    lane = lambda first: pl.ds(pl.multiple_of(first, 128), wide)
    mine = pl.ds(pl.multiple_of(row * 128, 128), 128)
    acro = pl.ds(pl.multiple_of((row + 1 - 2 * (row % 2)) * 128, 128), 128)
    sends = []
    def go(c):
        c.start()
        sends.append(c)
        return c
    sq = [go(remote(q_ref.at[:, lane((1 - core) * half + ch * wide)], Q.at[ch, 1, mine, :], qs.at[ch], qr.at[ch], sib)) for ch in range(chunks)]
    fr = go(remote(f_ref, F.at[1], fsem.at[0], fsem.at[1], sib))
    fl = pltpu.make_async_copy(f_ref, F.at[0], fsem.at[2])
    fl.start()
    for ch in range(chunks):
        Q[ch, 0, mine, :] = q_ref[:, lane(core * half + ch * wide)]
    def gat(ch, i, at, d):
        return go(remote(Q.at[ch, :, at, :], Q.at[ch, :, at, :], gs.at[ch, i], gr.at[ch, i], d))
    gx, gz = [], [[] for _ in range(chunks)]
    for ch in range(chunks):
        sq[ch].wait_recv()
        gx.append(gat(ch, 0, mine, across))
    def near(ch):
        for k in range(3):
            gz[ch].append(gat(ch, 1 + k, mine, zs[k]))
    def forward(ch):
        gx[ch].wait_recv()
        for k in range(3):
            gz[ch].append(gat(ch, 4 + k, acro, zs[k]))
    near(0)
    forward(0)
    ysend = [[] for _ in range(chunks)]
    xsend, psend = [None] * chunks, [None] * chunks
    xl = x % 2
    keep = pl.ds(pl.multiple_of(xl * 256, 256), 256)
    give = pl.ds(pl.multiple_of((1 - xl) * 256, 256), 256)
    def multiply(ch):
        for k in (2, 1, 3, 0):
            at = pl.ds(pl.multiple_of(((y + k) % 4) * 512, 512), 512)
            v = lax.dot_general(F[0, at, :], Q[ch, 0], NN, preferred_element_type=F32)
            v = v + lax.dot_general(F[1, at, :], Q[ch, 1], NN, preferred_element_type=F32)
            if k == 0:
                own[ch] = v
            else:
                S[ch, k - 1] = v.astype(BF)
                ysend[ch].append(go(remote(S.at[ch, k - 1], YR.at[ch, k - 1], ys.at[ch, k - 1], yr.at[ch, k - 1], yy[k - 1])))
    def add(ch):
        for c in ysend[ch]:
            c.wait_recv()
        def total(at):
            return own[ch, at, :] + ((YR[ch, 0, at, :].astype(F32) + YR[ch, 1, at, :].astype(F32)) + YR[ch, 2, at, :].astype(F32))
        XS[ch] = total(give)
        xsend[ch] = go(remote(XS.at[ch], XR.at[ch], xs.at[ch], xr.at[ch], beside))
        own[ch, keep, :] = total(keep)
    def finish(ch):
        xsend[ch].wait_recv()
        at = lane(core * half + ch * wide)
        P2[:, at] = (own[ch, keep, :] + XR[ch]).astype(BF)
        psend[ch] = go(remote(P2.at[:, at], P2.at[:, at], ps.at[ch], pr.at[ch], sib))
    for ch in range(chunks):
        if ch + 1 < chunks:
            near(ch + 1)
            forward(ch + 1)
        for c in gz[ch]:
            c.wait_recv()
        if ch == 0:
            fl.wait()
            fr.wait_recv()
        multiply(ch)
        if ch >= 1:
            add(ch - 1)
        if ch >= 2:
            finish(ch - 2)
    add(chunks - 1)
    finish(chunks - 2)
    finish(chunks - 1)
    for c in psend:
        c.wait_recv()
    p_ref[...] = P2[...]
    for c in sends:
        c.wait_send()

def product_rows(factor, slab, chunks=4):
    n = slab.shape[1]
    rows, cols = factor.shape
    wide = n // 2 // chunks
    dma = pltpu.SemaphoreType.DMA
    vm = pltpu.VMEM
    return pl.pallas_call(
        product_kernel,
        out_shape=jax.ShapeDtypeStruct((256, n), BF),
        in_specs=[pl.BlockSpec(memory_space=pl.ANY), pl.BlockSpec(memory_space=pltpu.VMEM)],
        out_specs=pl.BlockSpec(memory_space=pltpu.VMEM),
        scratch_shapes=[vm((2, rows, cols), BF), vm((chunks, 2, cols, wide), BF), vm((chunks, 3, 512, wide), BF),
            vm((chunks, 512, wide), F32), vm((chunks, 3, 512, wide), BF), vm((chunks, 256, wide), F32), vm((chunks, 256, wide), F32),
            vm((256, n), BF), dma((3,)), dma((chunks,)), dma((chunks,)), dma((chunks, 7)), dma((chunks, 7)),
            dma((chunks, 3)), dma((chunks, 3)), dma((chunks,)), dma((chunks,)), dma((chunks,)), dma((chunks,))],
        compiler_params=pltpu.CompilerParams(collective_id=0, has_side_effects=True, vmem_limit_bytes=48 * 2**20),
        name="product_rows",
    )(factor, slab)


def split(x):
    hi = x.astype(BF)
    return hi, (x - hi.astype(F32)).astype(BF)


def factor_block(d_ref, w_ref, width=16):
    n = 128
    rows_i = lax.broadcasted_iota(jnp.int32, (n, n), 0)
    cols_i = lax.broadcasted_iota(jnp.int32, (n, n), 1)
    w_ref[...] = jnp.where(rows_i == cols_i, 1.0, 0.0).astype(F32)
    np_ = n // width
    R, V = d_ref[:width, :], w_ref[:width, :]
    for p in range(np_):
        b0, m0, m1 = width * p, width * (p + 1), width * (p + 2)
        more = p < np_ - 1
        if more:
            N, NV = d_ref[m0:m1, :], w_ref[m0:m1, :]
            A = jnp.concatenate([R, N], 0)
            Z = jnp.concatenate([V, NV], 0)
        else:
            A, Z = R, V
        H = A.shape[0]
        C = [jnp.broadcast_to(A[:, b0 + b:b0 + b + 1], (H, n)) for b in range(width)]
        us, vs = [], []
        def sub(x, a):
            return x[a:a + 1, :]
        lo = 0
        for a in range(width):
            if a - lo == 8:
                C = [None if c is None else c[8:] for c in C]
                A, Z = A[8:], Z[8:]
                lo = a
            q = a - lo
            r = lax.rsqrt(sub(C[a], q))
            u, v = sub(A, q) * r, sub(Z, q) * r
            us.append(u); vs.append(v)
            ca = C[a] * r
            C[a] = None
            for b in range(a + 1, width):
                C[b] = C[b] - ca * jnp.broadcast_to(sub(ca, b - lo), ca.shape)
            A = A - ca * u
            Z = Z - ca * v
        U, W = jnp.concatenate(us, 0), jnp.concatenate(vs, 0)
        d_ref[b0:m0, :] = U
        w_ref[b0:m0, :] = W
        if more:
            R, V = A[width - lo:], Z[width - lo:]
        if p < np_ - 2:
            uh, ul = split(U)
            wh, wl = split(W)
            lhs = jnp.concatenate([uh, ul, uh], 0)
            rhs = jnp.concatenate([jnp.concatenate([uh, uh, ul], 0), jnp.concatenate([wh, wh, wl], 0)], 1)
            up = lax.dot_general(lhs, rhs, (((0,), (0,)), ((), ())), preferred_element_type=F32)
            d_ref[m1:, :] = d_ref[m1:, :] - up[m1:, :n]
            w_ref[m1:, :] = w_ref[m1:, :] - up[m1:, n:]
    d_ref[...] = jnp.where(rows_i <= cols_i, d_ref[...], 0.0)


B = 256
NT=(((1,),(1,)),((),()))
NN=(((1,),(0,)),((),()))
def mm(a,b,dims): return lax.dot_general(a,b,dims,preferred_element_type=F32)
def mm3(ah,al,bh,bl,dims): return mm(ah,bh,dims)+(mm(ah,bl,dims)+mm(al,bh,dims))
def mm3f(a,b,dims):
    ah,al=split(a); bh,bl=split(b)
    return mm3(ah,al,bh,bl,dims)

def factor_solve_kernel(g_ref, p_ref, m_ref, x_ref, y_ref, A, Lh, Ll, mh, ml, d_s, w_s, w_full, gsem):
    n = p_ref.shape[1]
    nb = n // B
    lens, starts = strips(n)
    copies = [
        pltpu.make_async_copy(
            g_ref.at[pl.ds(starts[c] * B, lens[c] * B), :],
            A.at[pl.ds((c // 2) * B, lens[c] * B), pl.ds(c * 128, 128)],
            gsem.at[c],
        )
        for c in range(len(lens))
    ]
    for c in copies: c.start()
    A[n:n+128, :] = p_ref[...].astype(F32)
    A[n+128:, :] = jnp.zeros((128, n), F32)
    mhi, mlo = split(m_ref[...])
    mh[...] = mhi; ml[...] = mlo
    def blk(i, k): return (pl.ds(pl.multiple_of(i*B, B), B), pl.ds(pl.multiple_of(k*B, B), B))
    for c in copies: c.wait()
    def step(k, carry):
        def row_tile(i, _):
            t = blk(i, k)
            def inner(j, acc):
                a, b = blk(i, j), blk(k, j)
                return acc - mm3(Lh[a], Ll[a], Lh[b], Ll[b], NT)
            A[t] = lax.fori_loop(0, k, inner, A[t])
            return 0
        lax.fori_loop(k, nb+1, row_tile, 0)
        kk = pl.multiple_of(k*B, B)
        h = 128
        q0, q1 = pl.ds(kk, h), pl.ds(kk+h, h)
        d_s[...] = A[q0, q0]
        factor_block(d_s, w_s)
        w0 = w_s[...]
        l00 = d_s[...].T
        l10 = mm3f(A[q1, q0], w0, NT)
        d_s[...] = A[q1, q1] - mm3f(l10, l10, NT)
        factor_block(d_s, w_s)
        w1 = w_s[...]
        l11 = d_s[...].T
        w10 = -mm3f(w1, mm3f(l10, w0, NN), NN)
        w_full[:h, :h] = w0
        w_full[:h, h:] = jnp.zeros((h, h), F32)
        w_full[h:, :h] = w10
        w_full[h:, h:] = w1
        for (r, c, v) in ((q0,q0,l00),(q0,q1,jnp.zeros((h,h),F32)),(q1,q0,l10),(q1,q1,l11)):
            hi, lo = split(v)
            Lh[r,c]=hi; Ll[r,c]=lo
        wh, wl = split(w_full[...])
        def panel(i, _):
            t = blk(i, k)
            ah, al = split(A[t])
            v = mm3(ah, al, wh, wl, NT)
            hi, lo = split(v)
            Lh[t] = hi; Ll[t] = lo
            return 0
        lax.fori_loop(k+1, nb+1, panel, 0)
        x_ref[:, pl.ds(kk, B)] = (Lh[n:n+128, pl.ds(kk, B)].astype(F32)+Ll[n:n+128, pl.ds(kk, B)].astype(F32)).astype(BF)
        def yt(i, acc):
            a = pl.ds(pl.multiple_of(i*B,B),B)
            t = blk(i, k)
            return acc + mm3(mh[:, a], ml[:, a], Lh[t], Ll[t], NN)
        y_ref[:, pl.ds(kk, B)] = lax.fori_loop(k, nb, yt, jnp.zeros((128, B), F32))
        return carry
    lax.fori_loop(0, nb, step, 0)

def factor_solve(g, p, m):
    n = p.shape[1]
    return pl.pallas_call(factor_solve_kernel,
        out_shape=[jax.ShapeDtypeStruct((128,n),BF), jax.ShapeDtypeStruct((128,n),F32)],
        in_specs=[pl.BlockSpec(memory_space=pl.ANY), pl.BlockSpec(memory_space=pltpu.VMEM), pl.BlockSpec(memory_space=pltpu.VMEM)],
        out_specs=[pl.BlockSpec(memory_space=pltpu.VMEM)]*2,
        scratch_shapes=[pltpu.VMEM((n+B,n),F32),pltpu.VMEM((n+B,n),BF),pltpu.VMEM((n+B,n),BF),pltpu.VMEM((128,n),BF),pltpu.VMEM((128,n),BF),
          pltpu.VMEM((128,128),F32),pltpu.VMEM((128,128),F32),pltpu.VMEM((B,B),F32),pltpu.SemaphoreType.DMA((n//128,))],
        compiler_params=pltpu.CompilerParams(vmem_limit_bytes=60*2**20),
        name="factor_solve")(g,p,m)


def body(factor, old_basis, first_moment):
    rows = product_rows(factor, old_basis)
    gram, product = gram_sum(rows)
    new_basis, rotated_moment = factor_solve(gram.reshape(-1, 128), product, first_moment)
    return (new_basis, rotated_moment)


def solution(mesh):
    placed = (P("row", "col"), P(("col", "row"), None), P(("col", "row"), None))
    return jax.shard_map(
        body,
        mesh=mesh,
        in_specs=placed,
        out_specs=(P(("col", "row"), None), P(("col", "row"), None)),
        check_vma=False,
    )
```

```python
import functools

import jax
import jax.numpy as jnp
from jax import lax
from jax.experimental import pallas as pl
from jax.experimental.pallas import tpu as pltpu
from jax.sharding import PartitionSpec as P

M = 16384
F32, BF = jnp.float32, jnp.bfloat16
MESH = pl.DeviceIdType.MESH
TN = (((0,), (0,)), ((), ()))

def coords():
    row, col = lax.axis_index("row"), lax.axis_index("col")
    return (row % 2) * 2 + (col // 2) % 2, col // 4, row // 2, col % 2

def device(x, y, z, core):
    return (z * 2 + x // 2, y * 4 + (x % 2) * 2 + core)

def links(x, y, z, core):
    near = lambda v: v + 1 - 2 * (v % 2)
    far = lambda v: 3 - v
    low = lambda v: (v + v // 2) % 2
    peers = [device(near(x), y, z, core), device(x, near(y), z, core), device(x, y, near(z), core),
             device(far(x), y, z, core), device(x, far(y), z, core), device(x, y, far(z), core)]
    bits = [low(x), low(y), low(z), x // 2, y // 2, z // 2]
    return peers, bits

def strips(n):
    lens = [n // 256 - c // 2 for c in range(n // 128)]
    starts = [sum(lens[:c]) for c in range(len(lens) + 1)]
    return lens, starts

def remote(src, dst, ssem, rsem, dev):
    return pltpu.make_async_remote_copy(src, dst, ssem, rsem, device_id=dev, device_id_type=MESH)

def gram_kernel(p_ref, g_ref, own_ref, W, RB, O, ss, rs, as_, ar, fs, fr, ls, ps, pr):
    x, y, z, core = coords()
    row, col = lax.axis_index("row"), lax.axis_index("col")
    peers, bits = links(x, y, z, core)
    sib = device(x, y, z, 1 - core)
    n = p_ref.shape[1]
    lens, starts = strips(n)
    parts, rows = W.shape[0], W.shape[1]
    tiles = rows // 256
    j = 2 * (col // 2) + 1 - core
    to = (j % 8, 2 * row + j // 8)
    i = (col % 2) * 8 + row
    frm = (col // 2, (i // 2) * 2 + 1 - i % 2)
    bar = pltpu.get_barrier_semaphore()
    for d in peers + [sib, frm]:
        pl.semaphore_signal(bar, inc=1, device_id=d, device_id_type=MESH)
    pl.semaphore_wait(bar, 8)

    def tile(s, u, _):
        U = core * (parts * tiles) + s * tiles + u
        c, st = 0, 0
        for q in range(1, len(lens)):
            past = (U >= starts[q]).astype(jnp.int32)
            c, st = c + past, st + past * lens[q - 1]
        i = U - st + c // 2
        a = p_ref[:, pl.ds(pl.multiple_of(i * 256, 256), 256)]
        b = p_ref[:, pl.ds(pl.multiple_of(c * 128, 128), 128)]
        W[s, pl.ds(pl.multiple_of(u * 256, 256), 256), :] = lax.dot_general(a, b, TN, preferred_element_type=F32) * (1.0 / M)
        return 0

    slab = remote(p_ref.at[pl.ds(pl.multiple_of((1 - core) * 128, 128), 128), :], own_ref, ps, pr, to)
    slab.start()

    off = [0] * parts
    steps = len(peers)
    sends = []
    def send(t, s):
        h = rows >> (t + 1)
        d = (s + t) % steps
        src = W.at[s, pl.ds(pl.multiple_of(off[s] + (1 - bits[d]) * h, 8), h), :]
        c = remote(src, RB.at[s, pl.ds(rows - 2 * h, h), :], ss.at[t, s], rs.at[t, s], peers[d])
        c.start()
        return c
    cur = []
    for s in range(parts):
        lax.fori_loop(0, tiles, functools.partial(tile, s), 0)
        cur.append(send(0, s))
    for t in range(steps):
        h = rows >> (t + 1)
        nxt = []
        for s in range(parts):
            cur[s].wait_recv()
            d = (s + t) % steps
            off[s] = off[s] + bits[d] * h
            at = pl.ds(pl.multiple_of(off[s], 8), h)
            if t < steps - 1:
                W[s, at, :] = W[s, at, :] + RB[s, pl.ds(rows - 2 * h, h), :]
                sends.append(cur[s])
                nxt.append(send(t + 1, s))
            else:
                O[s, at, :] = W[s, at, :] + RB[s, pl.ds(rows - 2 * h, h), :]
                sends.append(cur[s])
        cur = nxt
    tail = []
    def share(s, at, q):
        c = remote(O.at[s, at, :], g_ref.at[core, s, at, :], fs.at[q, s], fr.at[q, s], sib)
        l = pltpu.make_async_copy(O.at[s, at, :], g_ref.at[core, s, at, :], ls.at[q, s])
        c.start(); l.start()
        tail.append((c, l))
    def give(t, s):
        h = rows >> (t + 1)
        at = pl.ds(pl.multiple_of(off[s], 8), h)
        c = remote(O.at[s, at, :], O.at[s, at, :], as_.at[t, s], ar.at[t, s], peers[(s + t) % steps])
        c.start()
        return c
    cur = [give(steps - 1, s) for s in range(parts)]
    for t in range(steps - 1, -1, -1):
        h = rows >> (t + 1)
        nxt = []
        for s in range(parts):
            cur[s].wait_recv()
            b = bits[(s + t) % steps]
            got = off[s] + (1 - 2 * b) * h
            off[s] = off[s] - b * h
            sends.append(cur[s])
            if t > 0:
                nxt.append(give(t - 1, s))
            if t == 2:
                share(s, pl.ds(pl.multiple_of(off[s], 8), 2 * h), 2)
            elif t < 2:
                share(s, pl.ds(pl.multiple_of(got, 8), h), t)
        cur = nxt
    for c in sends:
        c.wait_send()
    for c, l in tail:
        l.wait()
        c.wait()
    slab.wait()

def gram_sum(p2):
    n = p2.shape[1]
    lens, starts = strips(n)
    rows = starts[-1] * 256 // 12
    dma = pltpu.SemaphoreType.DMA
    return pl.pallas_call(
        gram_kernel,
        out_shape=[jax.ShapeDtypeStruct((2, 6, rows, 128), F32), jax.ShapeDtypeStruct((128, n), BF)],
        in_specs=[pl.BlockSpec(memory_space=pltpu.VMEM)],
        out_specs=[pl.BlockSpec(memory_space=pl.ANY)] * 2,
        scratch_shapes=[pltpu.VMEM((6, rows, 128), F32)] * 3 + [dma((6, 6))] * 4 + [dma((3, 6))] * 3 + [dma(())] * 2,
        compiler_params=pltpu.CompilerParams(collective_id=1, has_side_effects=True, vmem_limit_bytes=40 * 2**20),
        name="gram_sum",
    )(p2)


def product_kernel(f_ref, q_ref, p_ref, F, Q, S, own, YR, XS, XR, P2, fsem, qs, qr, gs, gr, ys, yr, xs, xr, ps, pr):
    x, y, z, core = coords()
    row, col = lax.axis_index("row"), lax.axis_index("col")
    chunks, wide = Q.shape[0], Q.shape[3]
    half = chunks * wide
    sib = device(x, y, z, 1 - core)
    across = device((x + 2) % 4, y, z, core)
    beside = device(x + 1 - 2 * (x % 2), y, z, core)
    zs = [device(x, y, (z + k) % 4, core) for k in (1, 2, 3)]
    yy = [device(x, (y + k) % 4, z, core) for k in (1, 2, 3)]
    bar = pltpu.get_barrier_semaphore()
    for d in [sib, across, beside] + zs + yy:
        pl.semaphore_signal(bar, inc=1, device_id=d, device_id_type=MESH)
    pl.semaphore_wait(bar, 9)
    lane = lambda first: pl.ds(pl.multiple_of(first, 128), wide)
    mine = pl.ds(pl.multiple_of(row * 128, 128), 128)
    acro = pl.ds(pl.multiple_of((row + 1 - 2 * (row % 2)) * 128, 128), 128)
    sends = []
    def go(c):
        c.start()
        sends.append(c)
        return c
    sq = [go(remote(q_ref.at[:, lane((1 - core) * half + ch * wide)], Q.at[ch, 1, mine, :], qs.at[ch], qr.at[ch], sib)) for ch in range(chunks)]
    fr = go(remote(f_ref, F.at[1], fsem.at[0], fsem.at[1], sib))
    fl = pltpu.make_async_copy(f_ref, F.at[0], fsem.at[2])
    fl.start()
    for ch in range(chunks):
        Q[ch, 0, mine, :] = q_ref[:, lane(core * half + ch * wide)]
    def gat(ch, i, at, d):
        return go(remote(Q.at[ch, :, at, :], Q.at[ch, :, at, :], gs.at[ch, i], gr.at[ch, i], d))
    gx, gz = [], [[] for _ in range(chunks)]
    for ch in range(chunks):
        sq[ch].wait_recv()
        gx.append(gat(ch, 0, mine, across))
    def near(ch):
        for k in range(3):
            gz[ch].append(gat(ch, 1 + k, mine, zs[k]))
    def forward(ch):
        gx[ch].wait_recv()
        for k in range(3):
            gz[ch].append(gat(ch, 4 + k, acro, zs[k]))
    near(0)
    forward(0)
    ysend = [[] for _ in range(chunks)]
    xsend, psend = [None] * chunks, [None] * chunks
    xl = x % 2
    keep = pl.ds(pl.multiple_of(xl * 256, 256), 256)
    give = pl.ds(pl.multiple_of((1 - xl) * 256, 256), 256)
    def multiply(ch):
        for k in (2, 1, 3, 0):
            at = pl.ds(pl.multiple_of(((y + k) % 4) * 512, 512), 512)
            v = lax.dot_general(F[0, at, :], Q[ch, 0], NN, preferred_element_type=F32)
            v = v + lax.dot_general(F[1, at, :], Q[ch, 1], NN, preferred_element_type=F32)
            if k == 0:
                own[ch] = v
            else:
                S[ch, k - 1] = v.astype(BF)
                ysend[ch].append(go(remote(S.at[ch, k - 1], YR.at[ch, k - 1], ys.at[ch, k - 1], yr.at[ch, k - 1], yy[k - 1])))
    def add(ch):
        for c in ysend[ch]:
            c.wait_recv()
        def total(at):
            return own[ch, at, :] + ((YR[ch, 0, at, :].astype(F32) + YR[ch, 1, at, :].astype(F32)) + YR[ch, 2, at, :].astype(F32))
        XS[ch] = total(give)
        xsend[ch] = go(remote(XS.at[ch], XR.at[ch], xs.at[ch], xr.at[ch], beside))
        own[ch, keep, :] = total(keep)
    def finish(ch):
        xsend[ch].wait_recv()
        at = lane(core * half + ch * wide)
        P2[:, at] = (own[ch, keep, :] + XR[ch]).astype(BF)
        psend[ch] = go(remote(P2.at[:, at], P2.at[:, at], ps.at[ch], pr.at[ch], sib))
    for ch in range(chunks):
        if ch + 1 < chunks:
            near(ch + 1)
            forward(ch + 1)
        for c in gz[ch]:
            c.wait_recv()
        if ch == 0:
            fl.wait()
            fr.wait_recv()
        multiply(ch)
        if ch >= 1:
            add(ch - 1)
        if ch >= 2:
            finish(ch - 2)
    add(chunks - 1)
    finish(chunks - 2)
    finish(chunks - 1)
    for c in psend:
        c.wait_recv()
    p_ref[...] = P2[...]
    for c in sends:
        c.wait_send()

def product_rows(factor, slab, chunks=4):
    n = slab.shape[1]
    rows, cols = factor.shape
    wide = n // 2 // chunks
    dma = pltpu.SemaphoreType.DMA
    vm = pltpu.VMEM
    return pl.pallas_call(
        product_kernel,
        out_shape=jax.ShapeDtypeStruct((256, n), BF),
        in_specs=[pl.BlockSpec(memory_space=pl.ANY), pl.BlockSpec(memory_space=pltpu.VMEM)],
        out_specs=pl.BlockSpec(memory_space=pltpu.VMEM),
        scratch_shapes=[vm((2, rows, cols), BF), vm((chunks, 2, cols, wide), BF), vm((chunks, 3, 512, wide), BF),
            vm((chunks, 512, wide), F32), vm((chunks, 3, 512, wide), BF), vm((chunks, 256, wide), F32), vm((chunks, 256, wide), F32),
            vm((256, n), BF), dma((3,)), dma((chunks,)), dma((chunks,)), dma((chunks, 7)), dma((chunks, 7)),
            dma((chunks, 3)), dma((chunks, 3)), dma((chunks,)), dma((chunks,)), dma((chunks,)), dma((chunks,))],
        compiler_params=pltpu.CompilerParams(collective_id=0, has_side_effects=True, vmem_limit_bytes=48 * 2**20),
        name="product_rows",
    )(factor, slab)


def split(x):
    hi = x.astype(BF)
    return hi, (x - hi.astype(F32)).astype(BF)


def factor_block(d_ref, w_ref, slot, width=16):
    n = 128
    rows_i = lax.broadcasted_iota(jnp.int32, (n, n), 0)
    cols_i = lax.broadcasted_iota(jnp.int32, (n, n), 1)
    w_ref[...] = jnp.where(rows_i == cols_i, 1.0, 0.0).astype(F32)
    np_ = n // width
    R, V = d_ref[:width, :], w_ref[:width, :]
    for p in range(np_):
        b0, m0, m1 = width * p, width * (p + 1), width * (p + 2)
        more = p < np_ - 1
        if more:
            N, NV = d_ref[m0:m1, :], w_ref[m0:m1, :]
            A = jnp.concatenate([R, N], 0)
            Z = jnp.concatenate([V, NV], 0)
        else:
            A, Z = R, V
        H = A.shape[0]
        fin = slot(p)
        C = [jnp.broadcast_to(A[:, b0 + b:b0 + b + 1], (H, n)) for b in range(width)]
        us, vs = [], []
        def sub(x, a):
            return x[a:a + 1, :]
        lo = 0
        for a in range(width):
            if a - lo == 8:
                C = [None if c is None else c[8:] for c in C]
                A, Z = A[8:], Z[8:]
                lo = a
            q = a - lo
            r = lax.rsqrt(sub(C[a], q))
            u, v = sub(A, q) * r, sub(Z, q) * r
            us.append(u); vs.append(v)
            ca = C[a] * r
            C[a] = None
            for b in range(a + 1, width):
                C[b] = C[b] - ca * jnp.broadcast_to(sub(ca, b - lo), ca.shape)
            A = A - ca * u
            Z = Z - ca * v
        U, W = jnp.concatenate(us, 0), jnp.concatenate(vs, 0)
        d_ref[b0:m0, :] = U
        w_ref[b0:m0, :] = W
        if more:
            R, V = A[width - lo:], Z[width - lo:]
        fin()
        if p < np_ - 2:
            uh, ul = split(U)
            wh, wl = split(W)
            lhs = jnp.concatenate([uh, ul, uh], 0)
            rhs = jnp.concatenate([jnp.concatenate([uh, uh, ul], 0), jnp.concatenate([wh, wh, wl], 0)], 1)
            up = lax.dot_general(lhs, rhs, (((0,), (0,)), ((), ())), preferred_element_type=F32)
            d_ref[m1:, :] = d_ref[m1:, :] - up[m1:, :n]
            w_ref[m1:, :] = w_ref[m1:, :] - up[m1:, n:]
    d_ref[...] = jnp.where(rows_i <= cols_i, d_ref[...], 0.0)


B=256
NT=(((1,),(1,)),((),()))
NN=(((1,),(0,)),((),()))
def mm(a,b,dims): return lax.dot_general(a,b,dims,preferred_element_type=F32)
def mm3(ah,al,bh,bl,dims): return mm(ah,bh,dims)+(mm(ah,bl,dims)+mm(al,bh,dims))
def mm3f(a,b,dims):
    ah,al=split(a); bh,bl=split(b)
    return mm3(ah,al,bh,bl,dims)
def factor_solve_kernel(g_ref, p_ref, m_ref, x_ref, y_ref, A, Lh, Ll, mh, ml, ys, d_s, w_s, e_s, v_s, Wh, Wl, gsem):
    n = p_ref.shape[1]
    nb = n // B
    h = B // 2
    lens, starts = strips(n)
    copies = [
        pltpu.make_async_copy(
            g_ref.at[pl.ds(starts[c] * B, lens[c] * B), :],
            A.at[pl.ds((c // 2) * B, lens[c] * B), pl.ds(c * 128, 128)],
            gsem.at[c],
        )
        for c in range(len(lens))
    ]
    for c in copies: c.start()
    A[n:n+h, :] = p_ref[...].astype(F32)
    A[n+h:, :] = jnp.zeros((A.shape[0]-n-h, n), F32)
    for r in (Lh, Ll):
        r[n+B:, :] = jnp.zeros((B, n), BF)
    ys[...] = jnp.zeros_like(ys)
    Wh[...] = jnp.zeros_like(Wh); Wl[...] = jnp.zeros_like(Wl)
    mhi, mlo = split(m_ref[...])
    mh[...] = mhi; ml[...] = mlo
    bs = lambda i: pl.ds(pl.multiple_of(i*B, B), B)
    for c in copies: c.wait()
    def step(k, carry):
        kp = jnp.maximum(k-1, 0)
        kn = jnp.minimum(k+1, nb-1)
        def put(ref, r, c, v): ref[r, c] = v
        def update(i, c, j):
            r, cc, jj = bs(i), bs(c), bs(j)
            v = A[r, cc] - mm3(Lh[r, jj], Ll[r, jj], Lh[cc, jj], Ll[cc, jj], NT)
            return lambda: put(A, r, cc, v)
        def panel(i, c):
            r, cc = bs(i), bs(c)
            ah, al = split(A[r, cc])
            hi, lo = split(mm3(ah, al, Wh[...], Wl[...], NT))
            def fin():
                Lh[r, cc] = hi; Ll[r, cc] = lo
            return fin
        def moment(i, c, dst):
            r, cc, dd = bs(i), bs(c), bs(dst)
            v = ys[:, dd] + mm3(mh[:, r], ml[:, r], Lh[r, cc], Ll[r, cc], NN)
            return lambda: put(ys, slice(None), dd, v)
        def slot(s):
            fins = []
            if s < 8:
                if s < nb-1:
                    i = k+1+s
                    fins.append(panel(jnp.where((k >= 1) & (i <= nb), i, nb+1), kp))
                if s >= 1:
                    i = k+s
                    fins.append(update(jnp.where((k >= 1) & (i <= nb), i, nb+1), k, kp))
            else:
                for t in (2*(s-8), 2*(s-8)+1):
                    ok = (t < (nb-k)*k) & (k+1 < nb)
                    j = t // (nb-k)
                    i = k+1 + t - j*(nb-k)
                    fins.append(update(jnp.where(ok, i, nb+1), kn, jnp.where(ok, j, 0)))
                i = kp + (s-8)
                ok = (k >= 1) & (i < nb)
                fins.append(moment(jnp.where(ok, i, 0), kp, jnp.where(ok, kp, nb)))
            def fin():
                for f in fins: f()
            return fin
        kk = pl.multiple_of(k*B, B)
        q0, q1 = pl.ds(kk, h), pl.ds(kk+h, h)
        nx = bs(k+1)
        d_s[...] = A[q0, q0]
        factor_block(d_s, w_s, slot)
        w0h, w0l = split(w_s[...])
        l00 = d_s[...].T
        a10h, a10l = split(A[q1, q0])
        l10h, l10l = split(mm3(a10h, a10l, w0h, w0l, NT))
        e_s[...] = A[q1, q1] - mm3(l10h, l10l, l10h, l10l, NT)
        nh, nl = split(A[nx, q0])
        n0h, n0l = split(mm3(nh, nl, w0h, w0l, NT))
        n1 = A[nx, q1] - mm3(n0h, n0l, l10h, l10l, NT)
        uh, ul = split(mm3(l10h, l10l, w0h, w0l, NN))
        factor_block(e_s, v_s, lambda s: slot(s+8))
        w1h, w1l = split(v_s[...])
        n1h, n1l = split(n1)
        n1h, n1l = split(mm3(n1h, n1l, w1h, w1l, NT))
        Lh[nx, q0] = n0h; Ll[nx, q0] = n0l
        Lh[nx, q1] = n1h; Ll[nx, q1] = n1l
        cn = bs(kn)
        A[nx, cn] = A[nx, cn] - (mm3(n0h, n0l, n0h, n0l, NT) + mm3(n1h, n1l, n1h, n1l, NT))
        w10h, w10l = split(-mm3(w1h, w1l, uh, ul, NN))
        z = jnp.zeros((h, h), BF)
        for W, a, b, c in ((Wh, w0h, w10h, w1h), (Wl, w0l, w10l, w1l)):
            W[:h, :h] = a; W[h:, :h] = b; W[h:, h:] = c
        l0, l1 = split(l00), split(e_s[...].T)
        for L, a, b, c in ((Lh, l0[0], l10h, l1[0]), (Ll, l0[1], l10l, l1[1])):
            L[q0, q0] = a; L[q0, q1] = z; L[q1, q0] = b; L[q1, q1] = c
        x_ref[:, bs(kp)] = (Lh[n:n+h, bs(kp)].astype(F32) + Ll[n:n+h, bs(kp)].astype(F32)).astype(BF)
        return carry
    lax.fori_loop(0, nb, step, 0)
    last = slice(n-B, n)
    x_ref[:, last] = (Lh[n:n+h, last].astype(F32) + Ll[n:n+h, last].astype(F32)).astype(BF)
    y_ref[:, :n-B] = ys[:, :n-B]
    y_ref[:, last] = mm3(mh[:, last], ml[:, last], Lh[last, last], Ll[last, last], NN)

def factor_solve(g, p, m):
    n = p.shape[1]
    vm = pltpu.VMEM
    return pl.pallas_call(factor_solve_kernel,
        out_shape=[jax.ShapeDtypeStruct((128,n),BF), jax.ShapeDtypeStruct((128,n),F32)],
        in_specs=[pl.BlockSpec(memory_space=pl.ANY), pl.BlockSpec(memory_space=pltpu.VMEM), pl.BlockSpec(memory_space=pltpu.VMEM)],
        out_specs=[pl.BlockSpec(memory_space=pltpu.VMEM)]*2,
        scratch_shapes=[vm((n+2*B,n),F32),vm((n+2*B,n),BF),vm((n+2*B,n),BF),vm((128,n),BF),vm((128,n),BF),vm((128,n+B),F32),
          vm((128,128),F32),vm((128,128),F32),vm((128,128),F32),vm((128,128),F32),vm((B,B),BF),vm((B,B),BF),pltpu.SemaphoreType.DMA((n//128,))],
        compiler_params=pltpu.CompilerParams(vmem_limit_bytes=60*2**20),
        name="factor_solve")(g,p,m)


def body(factor, old_basis, first_moment):
    rows = product_rows(factor, old_basis)
    gram, product = gram_sum(rows)
    new_basis, rotated_moment = factor_solve(gram.reshape(-1, 128), product, first_moment)
    return (new_basis, rotated_moment)


def solution(mesh):
    placed = (P("row", "col"), P(("col", "row"), None), P(("col", "row"), None))
    return jax.shard_map(
        body,
        mesh=mesh,
        in_specs=placed,
        out_specs=(P(("col", "row"), None), P(("col", "row"), None)),
        check_vma=False,
    )
```

```python
import functools

import jax
import jax.numpy as jnp
from jax import lax
from jax.experimental import pallas as pl
from jax.experimental.pallas import tpu as pltpu
from jax.sharding import PartitionSpec as P

M = 16384
F32, BF = jnp.float32, jnp.bfloat16
MESH = pl.DeviceIdType.MESH
TN = (((0,), (0,)), ((), ()))

def coords():
    row, col = lax.axis_index("row"), lax.axis_index("col")
    return (row % 2) * 2 + (col // 2) % 2, col // 4, row // 2, col % 2

def device(x, y, z, core):
    return (z * 2 + x // 2, y * 4 + (x % 2) * 2 + core)

def links(x, y, z, core):
    near = lambda v: v + 1 - 2 * (v % 2)
    far = lambda v: 3 - v
    low = lambda v: (v + v // 2) % 2
    peers = [device(near(x), y, z, core), device(x, near(y), z, core), device(x, y, near(z), core),
             device(far(x), y, z, core), device(x, far(y), z, core), device(x, y, far(z), core)]
    bits = [low(x), low(y), low(z), x // 2, y // 2, z // 2]
    return peers, bits

def strips(n):
    lens = [n // 256 - c // 2 for c in range(n // 128)]
    starts = [sum(lens[:c]) for c in range(len(lens) + 1)]
    return lens, starts

def remote(src, dst, ssem, rsem, dev):
    return pltpu.make_async_remote_copy(src, dst, ssem, rsem, device_id=dev, device_id_type=MESH)

def gram_kernel(p_ref, g_ref, W, RB, O, ss, rs, as_, ar, fs, fr, ls):
    x, y, z, core = coords()
    peers, bits = links(x, y, z, core)
    sib = device(x, y, z, 1 - core)
    n = p_ref.shape[1]
    lens, starts = strips(n)
    parts, rows = W.shape[0], W.shape[1]
    tiles = rows // 256
    bar = pltpu.get_barrier_semaphore()
    for d in peers + [sib]:
        pl.semaphore_signal(bar, inc=1, device_id=d, device_id_type=MESH)
    pl.semaphore_wait(bar, 7)

    def tile(s, u, _):
        U = core * (parts * tiles) + s * tiles + u
        c, st = 0, 0
        for q in range(1, len(lens)):
            past = (U >= starts[q]).astype(jnp.int32)
            c, st = c + past, st + past * lens[q - 1]
        i = U - st + c // 2
        a = p_ref[:, pl.ds(pl.multiple_of(i * 256, 256), 256)]
        b = p_ref[:, pl.ds(pl.multiple_of(c * 128, 128), 128)]
        W[s, pl.ds(pl.multiple_of(u * 256, 256), 256), :] = lax.dot_general(a, b, TN, preferred_element_type=F32) * (1.0 / M)
        return 0

    off = [0] * parts
    steps = len(peers)
    sends = []
    def send(t, s):
        h = rows >> (t + 1)
        d = (s + t) % steps
        src = W.at[s, pl.ds(pl.multiple_of(off[s] + (1 - bits[d]) * h, 8), h), :]
        c = remote(src, RB.at[s, pl.ds(rows - 2 * h, h), :], ss.at[t, s], rs.at[t, s], peers[d])
        c.start()
        return c
    cur = []
    for s in range(parts):
        lax.fori_loop(0, tiles, functools.partial(tile, s), 0)
        cur.append(send(0, s))
    for t in range(steps):
        h = rows >> (t + 1)
        nxt = []
        for s in range(parts):
            cur[s].wait_recv()
            d = (s + t) % steps
            off[s] = off[s] + bits[d] * h
            at = pl.ds(pl.multiple_of(off[s], 8), h)
            if t < steps - 1:
                W[s, at, :] = W[s, at, :] + RB[s, pl.ds(rows - 2 * h, h), :]
                sends.append(cur[s])
                nxt.append(send(t + 1, s))
            else:
                O[s, at, :] = W[s, at, :] + RB[s, pl.ds(rows - 2 * h, h), :]
                sends.append(cur[s])
        cur = nxt
    tail = []
    def share(s, at, q):
        c = remote(O.at[s, at, :], g_ref.at[core, s, at, :], fs.at[q, s], fr.at[q, s], sib)
        l = pltpu.make_async_copy(O.at[s, at, :], g_ref.at[core, s, at, :], ls.at[q, s])
        c.start(); l.start()
        tail.append((c, l))
    def give(t, s):
        h = rows >> (t + 1)
        at = pl.ds(pl.multiple_of(off[s], 8), h)
        c = remote(O.at[s, at, :], O.at[s, at, :], as_.at[t, s], ar.at[t, s], peers[(s + t) % steps])
        c.start()
        return c
    cur = [give(steps - 1, s) for s in range(parts)]
    for t in range(steps - 1, -1, -1):
        h = rows >> (t + 1)
        nxt = []
        for s in range(parts):
            cur[s].wait_recv()
            b = bits[(s + t) % steps]
            got = off[s] + (1 - 2 * b) * h
            off[s] = off[s] - b * h
            sends.append(cur[s])
            if t > 0:
                nxt.append(give(t - 1, s))
            if t == 2:
                share(s, pl.ds(pl.multiple_of(off[s], 8), 2 * h), 2)
            elif t < 2:
                share(s, pl.ds(pl.multiple_of(got, 8), h), t)
        cur = nxt
    for c in sends:
        c.wait_send()
    for c, l in tail:
        l.wait()
        c.wait()

def gram_sum(p2):
    n = p2.shape[1]
    lens, starts = strips(n)
    rows = starts[-1] * 256 // 12
    dma = pltpu.SemaphoreType.DMA
    return pl.pallas_call(
        gram_kernel,
        out_shape=jax.ShapeDtypeStruct((2, 6, rows, 128), F32),
        in_specs=[pl.BlockSpec(memory_space=pltpu.VMEM)],
        out_specs=pl.BlockSpec(memory_space=pl.ANY),
        scratch_shapes=[pltpu.VMEM((6, rows, 128), F32)] * 3 + [dma((6, 6))] * 4 + [dma((3, 6))] * 3,
        compiler_params=pltpu.CompilerParams(collective_id=1, has_side_effects=True, vmem_limit_bytes=40 * 2**20),
        name="gram_sum",
    )(p2)


def product_kernel(f_ref, q_ref, p_ref, F, Q, S, own, YR, XS, XR, P2, fsem, qs, qr, gs, gr, ys, yr, xs, xr, ps, pr):
    x, y, z, core = coords()
    row, col = lax.axis_index("row"), lax.axis_index("col")
    chunks, wide = Q.shape[0], Q.shape[3]
    half = chunks * wide
    sib = device(x, y, z, 1 - core)
    across = device((x + 2) % 4, y, z, core)
    beside = device(x + 1 - 2 * (x % 2), y, z, core)
    zs = [device(x, y, (z + k) % 4, core) for k in (1, 2, 3)]
    yy = [device(x, (y + k) % 4, z, core) for k in (1, 2, 3)]
    bar = pltpu.get_barrier_semaphore()
    for d in [sib, across, beside] + zs + yy:
        pl.semaphore_signal(bar, inc=1, device_id=d, device_id_type=MESH)
    pl.semaphore_wait(bar, 9)
    lane = lambda first: pl.ds(pl.multiple_of(first, 128), wide)
    mine = pl.ds(pl.multiple_of(row * 128, 128), 128)
    acro = pl.ds(pl.multiple_of((row + 1 - 2 * (row % 2)) * 128, 128), 128)
    sends = []
    def go(c):
        c.start()
        sends.append(c)
        return c
    sq = [go(remote(q_ref.at[:, lane((1 - core) * half + ch * wide)], Q.at[ch, 1, mine, :], qs.at[ch], qr.at[ch], sib)) for ch in range(chunks)]
    fr = go(remote(f_ref, F.at[1], fsem.at[0], fsem.at[1], sib))
    fl = pltpu.make_async_copy(f_ref, F.at[0], fsem.at[2])
    fl.start()
    ql = [pltpu.make_async_copy(q_ref.at[:, lane(core * half + ch * wide)], Q.at[ch, 0, mine, :], qs.at[chunks + ch]) for ch in range(chunks)]
    for c in ql:
        c.start()
    def gat(ch, i, at, d):
        return go(remote(Q.at[ch, :, at, :], Q.at[ch, :, at, :], gs.at[ch, i], gr.at[ch, i], d))
    gx, gz = [], [[] for _ in range(chunks)]
    for ch in range(chunks):
        sq[ch].wait_recv()
        ql[ch].wait()
        gx.append(gat(ch, 0, mine, across))
    def near(ch):
        for k in range(3):
            gz[ch].append(gat(ch, 1 + k, mine, zs[k]))
    def forward(ch):
        gx[ch].wait_recv()
        for k in range(3):
            gz[ch].append(gat(ch, 4 + k, acro, zs[k]))
    near(0)
    forward(0)
    ysend = [[] for _ in range(chunks)]
    xsend, psend = [None] * chunks, [None] * chunks
    xl = x % 2
    keep = pl.ds(pl.multiple_of(xl * 256, 256), 256)
    give = pl.ds(pl.multiple_of((1 - xl) * 256, 256), 256)
    def multiply(ch):
        for k in (2, 1, 3, 0):
            at = pl.ds(pl.multiple_of(((y + k) % 4) * 512, 512), 512)
            v = lax.dot_general(F[0, at, :], Q[ch, 0], NN, preferred_element_type=F32)
            v = v + lax.dot_general(F[1, at, :], Q[ch, 1], NN, preferred_element_type=F32)
            if k == 0:
                own[ch] = v
            else:
                S[ch, k - 1] = v.astype(BF)
                ysend[ch].append(go(remote(S.at[ch, k - 1], YR.at[ch, k - 1], ys.at[ch, k - 1], yr.at[ch, k - 1], yy[k - 1])))
    def add(ch):
        for c in ysend[ch]:
            c.wait_recv()
        def total(at):
            return own[ch, at, :] + ((YR[ch, 0, at, :].astype(F32) + YR[ch, 1, at, :].astype(F32)) + YR[ch, 2, at, :].astype(F32))
        XS[ch] = total(give).astype(BF)
        xsend[ch] = go(remote(XS.at[ch], XR.at[ch], xs.at[ch], xr.at[ch], beside))
        own[ch, keep, :] = total(keep)
    def finish(ch):
        xsend[ch].wait_recv()
        at = lane(core * half + ch * wide)
        P2[:, at] = (own[ch, keep, :] + XR[ch].astype(F32)).astype(BF)
        psend[ch] = go(remote(P2.at[:, at], P2.at[:, at], ps.at[ch], pr.at[ch], sib))
    for ch in range(chunks):
        if ch + 1 < chunks:
            near(ch + 1)
            forward(ch + 1)
        for c in gz[ch]:
            c.wait_recv()
        if ch == 0:
            fl.wait()
            fr.wait_recv()
        multiply(ch)
        if ch >= 1:
            add(ch - 1)
        if ch >= 2:
            finish(ch - 2)
    add(chunks - 1)
    finish(chunks - 2)
    finish(chunks - 1)
    for c in psend:
        c.wait_recv()
    p_ref[...] = P2[...]
    for c in sends:
        c.wait_send()

def product_rows(factor, slab, chunks=8):
    n = slab.shape[1]
    rows, cols = factor.shape
    wide = n // 2 // chunks
    dma = pltpu.SemaphoreType.DMA
    vm = pltpu.VMEM
    return pl.pallas_call(
        product_kernel,
        out_shape=jax.ShapeDtypeStruct((256, n), BF),
        in_specs=[pl.BlockSpec(memory_space=pl.ANY)] * 2,
        out_specs=pl.BlockSpec(memory_space=pltpu.VMEM),
        scratch_shapes=[vm((2, rows, cols), BF), vm((chunks, 2, cols, wide), BF), vm((chunks, 3, 512, wide), BF),
            vm((chunks, 512, wide), F32), vm((chunks, 3, 512, wide), BF), vm((chunks, 256, wide), BF), vm((chunks, 256, wide), BF),
            vm((256, n), BF), dma((3,)), dma((2 * chunks,)), dma((chunks,)), dma((chunks, 7)), dma((chunks, 7)),
            dma((chunks, 3)), dma((chunks, 3)), dma((chunks,)), dma((chunks,)), dma((chunks,)), dma((chunks,))],
        compiler_params=pltpu.CompilerParams(collective_id=0, has_side_effects=True, vmem_limit_bytes=60 * 2**20),
        name="product_rows",
    )(factor, slab)


def split(x):
    hi = x.astype(BF)
    return hi, (x - hi.astype(F32)).astype(BF)


def factor_block(d_ref, w_ref, slot, width=16):
    n = 128
    rows_i = lax.broadcasted_iota(jnp.int32, (n, n), 0)
    cols_i = lax.broadcasted_iota(jnp.int32, (n, n), 1)
    w_ref[...] = jnp.where(rows_i == cols_i, 1.0, 0.0).astype(F32)
    np_ = n // width
    R, V = d_ref[:width, :], w_ref[:width, :]
    for p in range(np_):
        b0, m0, m1 = width * p, width * (p + 1), width * (p + 2)
        more = p < np_ - 1
        if more:
            N, NV = d_ref[m0:m1, :], w_ref[m0:m1, :]
            A = jnp.concatenate([R, N], 0)
            Z = jnp.concatenate([V, NV], 0)
        else:
            A, Z = R, V
        H = A.shape[0]
        fin = slot(p) if slot is not None else None
        C = [jnp.broadcast_to(A[:, b0 + b:b0 + b + 1], (H, n)) for b in range(width)]
        us, vs = [], []
        def sub(x, a):
            return x[a:a + 1, :]
        lo = 0
        for a in range(width):
            if a - lo == 8:
                C = [None if c is None else c[8:] for c in C]
                A, Z = A[8:], Z[8:]
                lo = a
            q = a - lo
            r = lax.rsqrt(sub(C[a], q))
            u, v = sub(A, q) * r, sub(Z, q) * r
            us.append(u); vs.append(v)
            ca = C[a] * r
            C[a] = None
            for b in range(a + 1, width):
                C[b] = C[b] - ca * jnp.broadcast_to(sub(ca, b - lo), ca.shape)
            A = A - ca * u
            Z = Z - ca * v
        U, W = jnp.concatenate(us, 0), jnp.concatenate(vs, 0)
        d_ref[b0:m0, :] = U
        w_ref[b0:m0, :] = W
        if more:
            R, V = A[width - lo:], Z[width - lo:]
        if fin is not None:
            fin()
        if p < np_ - 2:
            uh, ul = split(U)
            wh, wl = split(W)
            lhs = jnp.concatenate([uh, ul, uh], 0)
            rhs = jnp.concatenate([jnp.concatenate([uh, uh, ul], 0), jnp.concatenate([wh, wh, wl], 0)], 1)
            up = lax.dot_general(lhs, rhs, (((0,), (0,)), ((), ())), preferred_element_type=F32)
            d_ref[m1:, :] = d_ref[m1:, :] - up[m1:, :n]
            w_ref[m1:, :] = w_ref[m1:, :] - up[m1:, n:]
    d_ref[...] = jnp.where(rows_i <= cols_i, d_ref[...], 0.0)


B=256
NT=(((1,),(1,)),((),()))
NN=(((1,),(0,)),((),()))
def mm(a,b,dims): return lax.dot_general(a,b,dims,preferred_element_type=F32)
def mm3(ah,al,bh,bl,dims): return mm(ah,bh,dims)+(mm(ah,bl,dims)+mm(al,bh,dims))
def mm3f(a,b,dims):
    ah,al=split(a); bh,bl=split(b)
    return mm3(ah,al,bh,bl,dims)
def factor_solve_kernel(g_ref, p_ref, m_ref, x_ref, y_ref, A, Lh, Ll, mh, ml, ys, x_s, d_s, w_s, e_s, v_s, Wh, Wl, gsem, xs, xr):
    row, col = lax.axis_index("row"), lax.axis_index("col")
    core = col % 2
    i = 2 * (col // 2) + 1 - core
    to = (i % 8, 2 * row + i // 8)
    i = (col % 2) * 8 + row
    frm = (col // 2, (i // 2) * 2 + 1 - i % 2)
    bar = pltpu.get_barrier_semaphore()
    pl.semaphore_signal(bar, inc=1, device_id=frm, device_id_type=MESH)
    n = p_ref.shape[1]
    nb = n // B
    h = B // 2
    lens, starts = strips(n)
    copies = [
        pltpu.make_async_copy(
            g_ref.at[pl.ds(starts[c] * B, lens[c] * B), :],
            A.at[pl.ds((c // 2) * B, lens[c] * B), pl.ds(c * 128, 128)],
            gsem.at[c],
        )
        for c in range(len(lens))
    ]
    for c in copies: c.start()
    A[n:n+h, :] = p_ref[pl.ds(pl.multiple_of((1 - core) * h, h), h), :].astype(F32)
    A[n+h:, :] = jnp.zeros((A.shape[0]-n-h, n), F32)
    ys[...] = jnp.zeros_like(ys)
    Wh[...] = jnp.zeros_like(Wh); Wl[...] = jnp.zeros_like(Wl)
    mhi, mlo = split(m_ref[...])
    mh[...] = mhi; ml[...] = mlo
    bs = lambda i: pl.ds(pl.multiple_of(i*B, B), B)
    def step(k, carry, start=False):
        kp = jnp.maximum(k-1, 0)
        kn = jnp.minimum(k+1, nb-1)
        def put(ref, r, c, v): ref[r, c] = v
        def update(i, c, j):
            r, cc, jj = bs(i), bs(c), bs(j)
            v = A[r, cc] - mm3(Lh[r, jj], Ll[r, jj], Lh[cc, jj], Ll[cc, jj], NT)
            return lambda: put(A, r, cc, v)
        def panel(i, c):
            r, cc = bs(i), bs(c)
            ah, al = split(A[r, cc])
            hi, lo = split(mm3(ah, al, Wh[...], Wl[...], NT))
            def fin():
                Lh[r, cc] = hi; Ll[r, cc] = lo
            return fin
        def moment(i, c, dst):
            r, cc, dd = bs(i), bs(c), bs(dst)
            v = ys[:, dd] + mm3(mh[:, r], ml[:, r], Lh[r, cc], Ll[r, cc], NN)
            return lambda: put(ys, slice(None), dd, v)
        def slot(s):
            fins = []
            if s < 8:
                if s < nb-1:
                    i = k+1+s
                    fins.append(panel(jnp.where((k >= 1) & (i <= nb), i, 0), kp))
                if s >= 1:
                    i = k+s
                    fins.append(update(jnp.where((k >= 1) & (i <= nb), i, 0), k, kp))
            else:
                for t in (2*(s-8), 2*(s-8)+1):
                    ok = (t < (nb-k)*k) & (k+1 < nb)
                    j = t // (nb-k)
                    i = k+1 + t - j*(nb-k)
                    fins.append(update(jnp.where(ok, i, 0), kn, jnp.where(ok, j, 0)))
                i = kp + (s-8)
                ok = (k >= 1) & (i < nb)
                fins.append(moment(jnp.where(ok, i, 0), kp, jnp.where(ok, kp, nb)))
            def fin():
                for f in fins: f()
            return fin
        kk = pl.multiple_of(k*B, B)
        q0, q1 = pl.ds(kk, h), pl.ds(kk+h, h)
        nx = bs(k+1)
        d_s[...] = A[q0, q0]
        factor_block(d_s, w_s, None if start else slot)
        w0h, w0l = split(w_s[...])
        l00 = d_s[...].T
        a10h, a10l = split(A[q1, q0])
        l10h, l10l = split(mm3(a10h, a10l, w0h, w0l, NT))
        e_s[...] = A[q1, q1] - mm3(l10h, l10l, l10h, l10l, NT)
        nh, nl = split(A[nx, q0])
        n0h, n0l = split(mm3(nh, nl, w0h, w0l, NT))
        n1 = A[nx, q1] - mm3(n0h, n0l, l10h, l10l, NT)
        uh, ul = split(mm3(l10h, l10l, w0h, w0l, NN))
        factor_block(e_s, v_s, None if start else lambda s: slot(s+8))
        w1h, w1l = split(v_s[...])
        n1h, n1l = split(n1)
        n1h, n1l = split(mm3(n1h, n1l, w1h, w1l, NT))
        Lh[nx, q0] = n0h; Ll[nx, q0] = n0l
        Lh[nx, q1] = n1h; Ll[nx, q1] = n1l
        cn = bs(kn)
        A[nx, cn] = A[nx, cn] - (mm3(n0h, n0l, n0h, n0l, NT) + mm3(n1h, n1l, n1h, n1l, NT))
        w10h, w10l = split(-mm3(w1h, w1l, uh, ul, NN))
        z = jnp.zeros((h, h), BF)
        for W, a, b, c in ((Wh, w0h, w10h, w1h), (Wl, w0l, w10l, w1l)):
            W[:h, :h] = a; W[h:, :h] = b; W[h:, h:] = c
        l0, l1 = split(l00), split(e_s[...].T)
        for L, a, b, c in ((Lh, l0[0], l10h, l1[0]), (Ll, l0[1], l10l, l1[1])):
            L[q0, q0] = a; L[q0, q1] = z; L[q1, q0] = b; L[q1, q1] = c
        if not start:
            solved(kp)
        return carry
    def pass_on(c):
        at = bs(c)
        return remote(x_s.at[:, at], x_ref.at[:, at], xs.at[c], xr.at[c], to)
    def solved(c):
        at = bs(c)
        x_s[:, at] = (Lh[n:n+h, at].astype(F32) + Ll[n:n+h, at].astype(F32)).astype(BF)
        pass_on(c).start()
    for c in copies[:4]: c.wait()
    step(jnp.int32(0), 0, start=True)
    for c in copies[4:]: c.wait()
    pl.semaphore_wait(bar, 1)
    lax.fori_loop(1, nb, step, 0)
    solved(nb - 1)
    last = slice(n-B, n)
    y_ref[:, :n-B] = ys[:, :n-B]
    y_ref[:, last] = mm3(mh[:, last], ml[:, last], Lh[last, last], Ll[last, last], NN)
    for c in range(nb): pass_on(c).wait()

def factor_solve(g, p, m):
    n = p.shape[1]
    vm = pltpu.VMEM
    return pl.pallas_call(factor_solve_kernel,
        out_shape=[jax.ShapeDtypeStruct((128,n),BF), jax.ShapeDtypeStruct((128,n),F32)],
        in_specs=[pl.BlockSpec(memory_space=pl.ANY), pl.BlockSpec(memory_space=pltpu.VMEM), pl.BlockSpec(memory_space=pltpu.VMEM)],
        out_specs=[pl.BlockSpec(memory_space=pl.ANY), pl.BlockSpec(memory_space=pltpu.VMEM)],
        scratch_shapes=[vm((n+B,n),F32),vm((n+B,n),BF),vm((n+B,n),BF),vm((128,n),BF),vm((128,n),BF),vm((128,n+B),F32),vm((128,n),BF),
          vm((128,128),F32),vm((128,128),F32),vm((128,128),F32),vm((128,128),F32),vm((B,B),BF),vm((B,B),BF),pltpu.SemaphoreType.DMA((n//128,)),pltpu.SemaphoreType.DMA((n//B,)),pltpu.SemaphoreType.DMA((n//B,))],
        compiler_params=pltpu.CompilerParams(collective_id=2, has_side_effects=True, vmem_limit_bytes=54*2**20),
        name="factor_solve")(g,p,m)


def body(factor, old_basis, first_moment):
    rows = product_rows(factor, old_basis)
    gram = gram_sum(rows)
    new_basis, rotated_moment = factor_solve(gram.reshape(-1, 128), rows, first_moment)
    return (new_basis, rotated_moment)


def solution(mesh):
    placed = (P("row", "col"), P(("col", "row"), None), P(("col", "row"), None))
    return jax.shard_map(
        body,
        mesh=mesh,
        in_specs=placed,
        out_specs=(P(("col", "row"), None), P(("col", "row"), None)),
        check_vma=False,
    )
```

```python
import functools

import jax
import jax.numpy as jnp
from jax import lax
from jax.experimental import pallas as pl
from jax.experimental.pallas import tpu as pltpu
from jax.sharding import PartitionSpec as P

M = 16384
F32, BF = jnp.float32, jnp.bfloat16
MESH = pl.DeviceIdType.MESH
TN = (((0,), (0,)), ((), ()))

def coords():
    row, col = lax.axis_index("row"), lax.axis_index("col")
    return (row % 2) * 2 + (col // 2) % 2, col // 4, row // 2, col % 2

def device(x, y, z, core):
    return (z * 2 + x // 2, y * 4 + (x % 2) * 2 + core)

def links(x, y, z, core):
    near = lambda v: v + 1 - 2 * (v % 2)
    far = lambda v: 3 - v
    low = lambda v: (v + v // 2) % 2
    peers = [device(near(x), y, z, core), device(x, near(y), z, core), device(x, y, near(z), core),
             device(far(x), y, z, core), device(x, far(y), z, core), device(x, y, far(z), core)]
    bits = [low(x), low(y), low(z), x // 2, y // 2, z // 2]
    return peers, bits

def strips(n):
    lens = [n // 256 - c // 2 for c in range(n // 128)]
    starts = [sum(lens[:c]) for c in range(len(lens) + 1)]
    return lens, starts

def remote(src, dst, ssem, rsem, dev):
    return pltpu.make_async_remote_copy(src, dst, ssem, rsem, device_id=dev, device_id_type=MESH)

def gram_part(p_ref, g_ref, W, RB, O, PT, ss, rs, as_, ar, fs, fr, ls):
    x, y, z, core = coords()
    peers, bits = links(x, y, z, core)
    sib = device(x, y, z, 1 - core)
    n = p_ref.shape[1]
    lens, starts = strips(n)
    parts, rows = W.shape[0], W.shape[1]
    tiles = rows // 256
    for i in range(n // 256):
        PT[i * 256:(i + 1) * 256, :] = p_ref[:, i * 256:(i + 1) * 256].T

    def tile(s, u, _):
        U = core * (parts * tiles) + s * tiles + u
        c, st = 0, 0
        for q in range(1, len(lens)):
            past = (U >= starts[q]).astype(jnp.int32)
            c, st = c + past, st + past * lens[q - 1]
        i = U - st + c // 2
        a = PT[pl.ds(pl.multiple_of(i * 256, 256), 256), :]
        b = p_ref[:, pl.ds(pl.multiple_of(c * 128, 128), 128)]
        W[s, pl.ds(pl.multiple_of(u * 256, 256), 256), :] = jnp.dot(a, b, preferred_element_type=F32) * (1.0 / M)
        return 0

    off = [0] * parts
    steps = len(peers)
    sends = []
    def send(t, s):
        h = rows >> (t + 1)
        d = (s + t) % steps
        src = W.at[s, pl.ds(pl.multiple_of(off[s] + (1 - bits[d]) * h, 8), h), :]
        c = remote(src, RB.at[s, pl.ds(rows - 2 * h, h), :], ss.at[t, s], rs.at[t, s], peers[d])
        c.start()
        return c
    cur = []
    for s in range(parts):
        lax.fori_loop(0, tiles, functools.partial(tile, s), 0)
        cur.append(send(0, s))
    for t in range(steps):
        h = rows >> (t + 1)
        nxt = []
        for s in range(parts):
            cur[s].wait_recv()
            d = (s + t) % steps
            off[s] = off[s] + bits[d] * h
            at = pl.ds(pl.multiple_of(off[s], 8), h)
            if t < steps - 1:
                W[s, at, :] = W[s, at, :] + RB[s, pl.ds(rows - 2 * h, h), :]
                sends.append(cur[s])
                nxt.append(send(t + 1, s))
            else:
                O[s, at, :] = W[s, at, :] + RB[s, pl.ds(rows - 2 * h, h), :]
                sends.append(cur[s])
        cur = nxt
    tail = []
    def share(s, at, q):
        c = remote(O.at[s, at, :], g_ref.at[core, s, at, :], fs.at[q, s], fr.at[q, s], sib)
        l = pltpu.make_async_copy(O.at[s, at, :], g_ref.at[core, s, at, :], ls.at[q, s])
        c.start(); l.start()
        tail.append((c, l))
    def give(t, s):
        h = rows >> (t + 1)
        at = pl.ds(pl.multiple_of(off[s], 8), h)
        c = remote(O.at[s, at, :], O.at[s, at, :], as_.at[t, s], ar.at[t, s], peers[(s + t) % steps])
        c.start()
        return c
    cur = [give(steps - 1, s) for s in range(parts)]
    for t in range(steps - 1, -1, -1):
        h = rows >> (t + 1)
        nxt = []
        for s in range(parts):
            cur[s].wait_recv()
            b = bits[(s + t) % steps]
            got = off[s] + (1 - 2 * b) * h
            off[s] = off[s] - b * h
            sends.append(cur[s])
            if t > 0:
                nxt.append(give(t - 1, s))
            if t == 2:
                share(s, pl.ds(pl.multiple_of(off[s], 8), 2 * h), 2)
            elif t < 2:
                share(s, pl.ds(pl.multiple_of(got, 8), h), t)
        cur = nxt
    for c in sends:
        c.wait_send()
    for c, l in tail:
        l.wait()
        c.wait()

def product_part(f_ref, q_ref, p_ref, F, Q, S, own, YR, XS, XR, P2, fsem, qs, qr, gs, gr, ys, yr, xs, xr, ps, pr):
    x, y, z, core = coords()
    row, col = lax.axis_index("row"), lax.axis_index("col")
    chunks, wide = Q.shape[0], Q.shape[3]
    half = chunks * wide
    sib = device(x, y, z, 1 - core)
    across = device((x + 2) % 4, y, z, core)
    beside = device(x + 1 - 2 * (x % 2), y, z, core)
    behind = device(3 - x, y, z, core)
    zs = [device(x, y, (z + k) % 4, core) for k in (1, 2, 3)]
    yy = [device(x, (y + k) % 4, z, core) for k in (1, 2, 3)]
    bar = pltpu.get_barrier_semaphore()
    for d in [sib, across, beside, behind] + zs + yy:
        pl.semaphore_signal(bar, inc=1, device_id=d, device_id_type=MESH)
    pl.semaphore_wait(bar, 10)
    lane = lambda first: pl.ds(pl.multiple_of(first, 128), wide)
    mine = pl.ds(pl.multiple_of(row * 128, 128), 128)
    acro = pl.ds(pl.multiple_of((row + 1 - 2 * (row % 2)) * 128, 128), 128)
    sends = []
    def go(c):
        c.start()
        sends.append(c)
        return c
    sq = [go(remote(q_ref.at[:, lane((1 - core) * half + ch * wide)], Q.at[ch, 1, mine, :], qs.at[ch], qr.at[ch], sib)) for ch in range(chunks)]
    fr = go(remote(f_ref, F.at[1], fsem.at[0], fsem.at[1], sib))
    fl = pltpu.make_async_copy(f_ref, F.at[0], fsem.at[2])
    fl.start()
    ql = [pltpu.make_async_copy(q_ref.at[:, lane(core * half + ch * wide)], Q.at[ch, 0, mine, :], qs.at[chunks + ch]) for ch in range(chunks)]
    for c in ql:
        c.start()
    def gat(ch, i, at, d):
        return go(remote(Q.at[ch, :, at, :], Q.at[ch, :, at, :], gs.at[ch, i], gr.at[ch, i], d))
    gx, gz = [], [[] for _ in range(chunks)]
    for ch in range(chunks):
        sq[ch].wait_recv()
        ql[ch].wait()
        gx.append(gat(ch, 0, mine, across))
    def near(ch):
        for k in range(3):
            gz[ch].append(gat(ch, 1 + k, mine, zs[k]))
    def forward(ch):
        gx[ch].wait_recv()
        for k in range(3):
            gz[ch].append(gat(ch, 4 + k, acro, zs[k]))
    near(0)
    forward(0)
    ysend = [[] for _ in range(chunks)]
    xsend, psend = [None] * chunks, [None] * chunks
    xl = x % 2
    keep = pl.ds(pl.multiple_of(xl * 256, 256), 256)
    give = pl.ds(pl.multiple_of((1 - xl) * 256, 256), 256)
    def multiply(ch):
        for k in (2, 1, 3, 0):
            at = pl.ds(pl.multiple_of(((y + k) % 4) * 512, 512), 512)
            v = lax.dot_general(F[0, at, :], Q[ch, 0], NN, preferred_element_type=F32)
            v = v + lax.dot_general(F[1, at, :], Q[ch, 1], NN, preferred_element_type=F32)
            if k == 0:
                own[ch] = v
            else:
                S[ch, k - 1] = v.astype(BF)
                ysend[ch].append(go(remote(S.at[ch, k - 1], YR.at[ch, k - 1], ys.at[ch, k - 1], yr.at[ch, k - 1], yy[k - 1])))
    def add(ch):
        for c in ysend[ch]:
            c.wait_recv()
        def total(at):
            return own[ch, at, :] + ((YR[ch, 0, at, :].astype(F32) + YR[ch, 1, at, :].astype(F32)) + YR[ch, 2, at, :].astype(F32))
        XS[ch] = total(give).astype(BF)
        xsend[ch] = go(remote(XS.at[ch], XR.at[ch], xs.at[ch], xr.at[ch], beside))
        own[ch, keep, :] = total(keep)
    def finish(ch):
        xsend[ch].wait_recv()
        at = lane(core * half + ch * wide)
        P2[:, at] = (own[ch, keep, :] + XR[ch].astype(F32)).astype(BF)
        psend[ch] = go(remote(P2.at[:, at], P2.at[:, at], ps.at[ch], pr.at[ch], sib))
    for ch in range(chunks):
        if ch + 1 < chunks:
            near(ch + 1)
            forward(ch + 1)
        for c in gz[ch]:
            c.wait_recv()
        if ch == 0:
            fl.wait()
            fr.wait_recv()
        multiply(ch)
        if ch >= 1:
            add(ch - 1)
        if ch >= 2:
            finish(ch - 2)
    add(chunks - 1)
    finish(chunks - 2)
    finish(chunks - 1)
    for c in psend:
        c.wait_recv()
    p_ref[...] = P2[...]
    for c in sends:
        c.wait_send()

def product_gram_kernel(f_ref, q_ref, g_ref, p_ref, *scratch):
    product_part(f_ref, q_ref, p_ref, *scratch[:19])
    gram_part(scratch[7], g_ref, *scratch[19:])


def product_gram(factor, slab, chunks=8):
    n = slab.shape[1]
    rows, cols = factor.shape
    wide = n // 2 // chunks
    _, starts = strips(n)
    tall = starts[-1] * 256 // 12
    dma = pltpu.SemaphoreType.DMA
    vm = pltpu.VMEM
    return pl.pallas_call(
        product_gram_kernel,
        out_shape=[jax.ShapeDtypeStruct((2, 6, tall, 128), F32), jax.ShapeDtypeStruct((256, n), BF)],
        in_specs=[pl.BlockSpec(memory_space=pl.ANY)] * 2,
        out_specs=[pl.BlockSpec(memory_space=pl.ANY), pl.BlockSpec(memory_space=pltpu.VMEM)],
        scratch_shapes=[
            vm((2, rows, cols), BF), vm((chunks, 2, cols, wide), BF), vm((chunks, 3, 512, wide), BF), vm((chunks, 512, wide), F32),
            vm((chunks, 3, 512, wide), BF), vm((chunks, 256, wide), BF), vm((chunks, 256, wide), BF), vm((256, n), BF),
            dma((3,)), dma((2 * chunks,)), dma((chunks,)), dma((chunks, 7)), dma((chunks, 7)), dma((chunks, 3)), dma((chunks, 3)),
            dma((chunks,)), dma((chunks,)), dma((chunks,)), dma((chunks,)),
        ] + [vm((6, tall, 128), F32)] * 3 + [vm((n, 256), BF)] + [dma((6, 6))] * 4 + [dma((3, 6))] * 3,
        compiler_params=pltpu.CompilerParams(collective_id=0, has_side_effects=True, vmem_limit_bytes=60 * 2**20),
        name="product_gram",
    )(factor, slab)


def split(x):
    hi = x.astype(BF)
    return hi, (x - hi.astype(F32)).astype(BF)


def factor_block(d_ref, w_ref, slot, width=16):
    n = 128
    rows_i = lax.broadcasted_iota(jnp.int32, (n, n), 0)
    cols_i = lax.broadcasted_iota(jnp.int32, (n, n), 1)
    w_ref[...] = jnp.where(rows_i == cols_i, 1.0, 0.0).astype(F32)
    np_ = n // width
    R, V = d_ref[:width, :], w_ref[:width, :]
    for p in range(np_):
        b0, m0, m1 = width * p, width * (p + 1), width * (p + 2)
        more = p < np_ - 1
        if more:
            N, NV = d_ref[m0:m1, :], w_ref[m0:m1, :]
            A = jnp.concatenate([R, N], 0)
            Z = jnp.concatenate([V, NV], 0)
        else:
            A, Z = R, V
        H = A.shape[0]
        fin = slot(p) if slot is not None else None
        C = [jnp.broadcast_to(A[:, b0 + b:b0 + b + 1], (H, n)) for b in range(width)]
        us, vs = [], []
        def sub(x, a):
            return x[a:a + 1, :]
        lo = 0
        for a in range(width):
            if a - lo == 8:
                C = [None if c is None else c[8:] for c in C]
                A, Z = A[8:], Z[8:]
                lo = a
            q = a - lo
            r = lax.rsqrt(sub(C[a], q))
            u, v = sub(A, q) * r, sub(Z, q) * r
            us.append(u); vs.append(v)
            ca = C[a] * r
            C[a] = None
            for b in range(a + 1, width):
                C[b] = C[b] - ca * jnp.broadcast_to(sub(ca, b - lo), ca.shape)
            A = A - ca * u
            Z = Z - ca * v
        U, W = jnp.concatenate(us, 0), jnp.concatenate(vs, 0)
        d_ref[b0:m0, :] = U
        w_ref[b0:m0, :] = W
        if more:
            R, V = A[width - lo:], Z[width - lo:]
        if fin is not None:
            fin()
        if p < np_ - 2:
            uh, ul = split(U)
            wh, wl = split(W)
            lhs = jnp.concatenate([uh, ul, uh], 0)
            rhs = jnp.concatenate([jnp.concatenate([uh, uh, ul], 0), jnp.concatenate([wh, wh, wl], 0)], 1)
            up = lax.dot_general(lhs, rhs, (((0,), (0,)), ((), ())), preferred_element_type=F32)
            d_ref[m1:, :] = d_ref[m1:, :] - up[m1:, :n]
            w_ref[m1:, :] = w_ref[m1:, :] - up[m1:, n:]
    d_ref[...] = jnp.where(rows_i <= cols_i, d_ref[...], 0.0)


B=256
NT=(((1,),(1,)),((),()))
NN=(((1,),(0,)),((),()))
def mm(a,b,dims): return lax.dot_general(a,b,dims,preferred_element_type=F32)
def mm3(ah,al,bh,bl,dims): return mm(ah,bh,dims)+(mm(ah,bl,dims)+mm(al,bh,dims))
def mm3f(a,b,dims):
    ah,al=split(a); bh,bl=split(b)
    return mm3(ah,al,bh,bl,dims)
def factor_solve_kernel(g_ref, p_ref, m_ref, x_ref, y_ref, A, Lh, Ll, mh, ml, ys, x_s, d_s, w_s, e_s, v_s, Wh, Wl, gsem, xs, xr):
    row, col = lax.axis_index("row"), lax.axis_index("col")
    core = col % 2
    i = 2 * (col // 2) + 1 - core
    to = (i % 8, 2 * row + i // 8)
    i = (col % 2) * 8 + row
    frm = (col // 2, (i // 2) * 2 + 1 - i % 2)
    bar = pltpu.get_barrier_semaphore()
    pl.semaphore_signal(bar, inc=1, device_id=frm, device_id_type=MESH)
    n = p_ref.shape[1]
    nb = n // B
    h = B // 2
    lens, starts = strips(n)
    copies = [
        pltpu.make_async_copy(
            g_ref.at[pl.ds(starts[c] * B, lens[c] * B), :],
            A.at[pl.ds((c // 2) * B, lens[c] * B), pl.ds(c * 128, 128)],
            gsem.at[c],
        )
        for c in range(len(lens))
    ]
    for c in copies: c.start()
    A[n:n+h, :] = p_ref[pl.ds(pl.multiple_of((1 - core) * h, h), h), :].astype(F32)
    A[n+h:, :] = jnp.zeros((A.shape[0]-n-h, n), F32)
    ys[...] = jnp.zeros_like(ys)
    Wh[...] = jnp.zeros_like(Wh); Wl[...] = jnp.zeros_like(Wl)
    mhi, mlo = split(m_ref[...])
    mh[...] = mhi; ml[...] = mlo
    bs = lambda i: pl.ds(pl.multiple_of(i*B, B), B)
    def step(k, carry, start=False):
        kp = jnp.maximum(k-1, 0)
        kn = jnp.minimum(k+1, nb-1)
        def put(ref, r, c, v): ref[r, c] = v
        def update(i, c, j):
            r, cc, jj = bs(i), bs(c), bs(j)
            v = A[r, cc] - mm3(Lh[r, jj], Ll[r, jj], Lh[cc, jj], Ll[cc, jj], NT)
            return lambda: put(A, r, cc, v)
        def panel(i, c):
            r, cc = bs(i), bs(c)
            ah, al = split(A[r, cc])
            hi, lo = split(mm3(ah, al, Wh[...], Wl[...], NT))
            def fin():
                Lh[r, cc] = hi; Ll[r, cc] = lo
            return fin
        def moment(i, c, dst):
            r, cc, dd = bs(i), bs(c), bs(dst)
            v = ys[:, dd] + mm3(mh[:, r], ml[:, r], Lh[r, cc], Ll[r, cc], NN)
            return lambda: put(ys, slice(None), dd, v)
        def slot(s):
            fins = []
            if s < 8:
                if s < nb-1:
                    i = k+1+s
                    fins.append(panel(jnp.where((k >= 1) & (i <= nb), i, 0), kp))
                if s >= 1:
                    i = k+s
                    fins.append(update(jnp.where((k >= 1) & (i <= nb), i, 0), k, kp))
            else:
                for t in (2*(s-8), 2*(s-8)+1):
                    ok = (t < (nb-k)*k) & (k+1 < nb)
                    j = t // (nb-k)
                    i = k+1 + t - j*(nb-k)
                    fins.append(update(jnp.where(ok, i, 0), kn, jnp.where(ok, j, 0)))
                i = kp + (s-8)
                ok = (k >= 1) & (i < nb)
                fins.append(moment(jnp.where(ok, i, 0), kp, jnp.where(ok, kp, nb)))
            def fin():
                for f in fins: f()
            return fin
        kk = pl.multiple_of(k*B, B)
        q0, q1 = pl.ds(kk, h), pl.ds(kk+h, h)
        nx = bs(k+1)
        d_s[...] = A[q0, q0]
        factor_block(d_s, w_s, None if start else slot)
        w0h, w0l = split(w_s[...])
        l00 = d_s[...].T
        a10h, a10l = split(A[q1, q0])
        l10h, l10l = split(mm3(a10h, a10l, w0h, w0l, NT))
        e_s[...] = A[q1, q1] - mm3(l10h, l10l, l10h, l10l, NT)
        nh, nl = split(A[nx, q0])
        n0h, n0l = split(mm3(nh, nl, w0h, w0l, NT))
        n1 = A[nx, q1] - mm3(n0h, n0l, l10h, l10l, NT)
        uh, ul = split(mm3(l10h, l10l, w0h, w0l, NN))
        factor_block(e_s, v_s, None if start else lambda s: slot(s+8))
        w1h, w1l = split(v_s[...])
        n1h, n1l = split(n1)
        n1h, n1l = split(mm3(n1h, n1l, w1h, w1l, NT))
        Lh[nx, q0] = n0h; Ll[nx, q0] = n0l
        Lh[nx, q1] = n1h; Ll[nx, q1] = n1l
        cn = bs(kn)
        A[nx, cn] = A[nx, cn] - (mm3(n0h, n0l, n0h, n0l, NT) + mm3(n1h, n1l, n1h, n1l, NT))
        w10h, w10l = split(-mm3(w1h, w1l, uh, ul, NN))
        z = jnp.zeros((h, h), BF)
        for W, a, b, c in ((Wh, w0h, w10h, w1h), (Wl, w0l, w10l, w1l)):
            W[:h, :h] = a; W[h:, :h] = b; W[h:, h:] = c
        l0, l1 = split(l00), split(e_s[...].T)
        for L, a, b, c in ((Lh, l0[0], l10h, l1[0]), (Ll, l0[1], l10l, l1[1])):
            L[q0, q0] = a; L[q0, q1] = z; L[q1, q0] = b; L[q1, q1] = c
        if not start:
            solved(kp)
        return carry
    def pass_on(c):
        at = bs(c)
        return remote(x_s.at[:, at], x_ref.at[:, at], xs.at[c], xr.at[c], to)
    def solved(c):
        at = bs(c)
        x_s[:, at] = (Lh[n:n+h, at].astype(F32) + Ll[n:n+h, at].astype(F32)).astype(BF)
        pass_on(c).start()
    for c in copies[:4]: c.wait()
    step(jnp.int32(0), 0, start=True)
    for c in copies[4:]: c.wait()
    pl.semaphore_wait(bar, 1)
    lax.fori_loop(1, nb, step, 0)
    solved(nb - 1)
    last = slice(n-B, n)
    y_ref[:, :n-B] = ys[:, :n-B]
    y_ref[:, last] = mm3(mh[:, last], ml[:, last], Lh[last, last], Ll[last, last], NN)
    for c in range(nb): pass_on(c).wait()

def factor_solve(g, p, m):
    n = p.shape[1]
    vm = pltpu.VMEM
    return pl.pallas_call(factor_solve_kernel,
        out_shape=[jax.ShapeDtypeStruct((128,n),BF), jax.ShapeDtypeStruct((128,n),F32)],
        in_specs=[pl.BlockSpec(memory_space=pl.ANY), pl.BlockSpec(memory_space=pltpu.VMEM), pl.BlockSpec(memory_space=pltpu.VMEM)],
        out_specs=[pl.BlockSpec(memory_space=pl.ANY), pl.BlockSpec(memory_space=pltpu.VMEM)],
        scratch_shapes=[vm((n+B,n),F32),vm((n+B,n),BF),vm((n+B,n),BF),vm((128,n),BF),vm((128,n),BF),vm((128,n+B),F32),vm((128,n),BF),
          vm((128,128),F32),vm((128,128),F32),vm((128,128),F32),vm((128,128),F32),vm((B,B),BF),vm((B,B),BF),pltpu.SemaphoreType.DMA((n//128,)),pltpu.SemaphoreType.DMA((n//B,)),pltpu.SemaphoreType.DMA((n//B,))],
        compiler_params=pltpu.CompilerParams(collective_id=1, has_side_effects=True, vmem_limit_bytes=54*2**20),
        name="factor_solve")(g,p,m)


def body(factor, old_basis, first_moment):
    gram, rows = product_gram(factor, old_basis)
    new_basis, rotated_moment = factor_solve(gram.reshape(-1, 128), rows, first_moment)
    return (new_basis, rotated_moment)


def solution(mesh):
    placed = (P("row", "col"), P(("col", "row"), None), P(("col", "row"), None))
    return jax.shard_map(
        body,
        mesh=mesh,
        in_specs=placed,
        out_specs=(P(("col", "row"), None), P(("col", "row"), None)),
        check_vma=False,
    )
```

```python
import functools

import jax
import jax.numpy as jnp
from jax import lax
from jax.experimental import pallas as pl
from jax.experimental.pallas import tpu as pltpu
from jax.sharding import PartitionSpec as P

M = 16384
F32, BF = jnp.float32, jnp.bfloat16
MESH = pl.DeviceIdType.MESH
TN = (((0,), (0,)), ((), ()))

def coords():
    row, col = lax.axis_index("row"), lax.axis_index("col")
    return (row % 2) * 2 + (col // 2) % 2, col // 4, row // 2, col % 2

def device(x, y, z, core):
    return (z * 2 + x // 2, y * 4 + (x % 2) * 2 + core)

def links(x, y, z, core):
    near = lambda v: v + 1 - 2 * (v % 2)
    far = lambda v: 3 - v
    low = lambda v: (v + v // 2) % 2
    peers = [device(near(x), y, z, core), device(x, near(y), z, core), device(x, y, near(z), core),
             device(far(x), y, z, core), device(x, far(y), z, core), device(x, y, far(z), core)]
    bits = [low(x), low(y), low(z), x // 2, y // 2, z // 2]
    return peers, bits

def strips(n):
    lens = [n // 256 - c // 2 for c in range(n // 128)]
    starts = [sum(lens[:c]) for c in range(len(lens) + 1)]
    return lens, starts

def remote(src, dst, ssem, rsem, dev):
    return pltpu.make_async_remote_copy(src, dst, ssem, rsem, device_id=dev, device_id_type=MESH)

def gram_part(p_ref, g_ref, W, RB, O, PT, ss, rs, as_, ar, fs, fr, ls):
    x, y, z, core = coords()
    peers, bits = links(x, y, z, core)
    sib = device(x, y, z, 1 - core)
    n = p_ref.shape[1]
    lens, starts = strips(n)
    parts, rows = W.shape[0], W.shape[1]
    tiles = rows // 256
    for i in range(n // 256):
        PT[i * 256:(i + 1) * 256, :] = p_ref[:, i * 256:(i + 1) * 256].T

    def tile(s, u, _):
        U = core * (parts * tiles) + s * tiles + u
        c, st = 0, 0
        for q in range(1, len(lens)):
            past = (U >= starts[q]).astype(jnp.int32)
            c, st = c + past, st + past * lens[q - 1]
        i = U - st + c // 2
        a = PT[pl.ds(pl.multiple_of(i * 256, 256), 256), :]
        b = p_ref[:, pl.ds(pl.multiple_of(c * 128, 128), 128)]
        W[s, pl.ds(pl.multiple_of(u * 256, 256), 256), :] = jnp.dot(a, b, preferred_element_type=F32) * (1.0 / M)
        return 0

    off = [0] * parts
    steps = len(peers)
    sends = []
    def send(t, s):
        h = rows >> (t + 1)
        d = (s + t) % steps
        src = W.at[s, pl.ds(pl.multiple_of(off[s] + (1 - bits[d]) * h, 8), h), :]
        c = remote(src, RB.at[s, pl.ds(rows - 2 * h, h), :], ss.at[t, s], rs.at[t, s], peers[d])
        c.start()
        return c
    cur = []
    for s in range(parts):
        lax.fori_loop(0, tiles, functools.partial(tile, s), 0)
        cur.append(send(0, s))
    for t in range(steps):
        h = rows >> (t + 1)
        nxt = []
        for s in range(parts):
            cur[s].wait_recv()
            d = (s + t) % steps
            off[s] = off[s] + bits[d] * h
            at = pl.ds(pl.multiple_of(off[s], 8), h)
            if t < steps - 1:
                W[s, at, :] = W[s, at, :] + RB[s, pl.ds(rows - 2 * h, h), :]
                sends.append(cur[s])
                nxt.append(send(t + 1, s))
            else:
                O[s, at, :] = W[s, at, :] + RB[s, pl.ds(rows - 2 * h, h), :]
                sends.append(cur[s])
        cur = nxt
    tail = []
    def share(s, at, q):
        c = remote(O.at[s, at, :], g_ref.at[core, s, at, :], fs.at[q, s], fr.at[q, s], sib)
        l = pltpu.make_async_copy(O.at[s, at, :], g_ref.at[core, s, at, :], ls.at[q, s])
        c.start(); l.start()
        tail.append((c, l))
    def give(t, s):
        h = rows >> (t + 1)
        at = pl.ds(pl.multiple_of(off[s], 8), h)
        c = remote(O.at[s, at, :], O.at[s, at, :], as_.at[t, s], ar.at[t, s], peers[(s + t) % steps])
        c.start()
        return c
    cur = [give(steps - 1, s) for s in range(parts)]
    for t in range(steps - 1, -1, -1):
        h = rows >> (t + 1)
        nxt = []
        for s in range(parts):
            cur[s].wait_recv()
            b = bits[(s + t) % steps]
            got = off[s] + (1 - 2 * b) * h
            off[s] = off[s] - b * h
            sends.append(cur[s])
            if t > 0:
                nxt.append(give(t - 1, s))
            if t == 2:
                share(s, pl.ds(pl.multiple_of(off[s], 8), 2 * h), 2)
            elif t < 2:
                share(s, pl.ds(pl.multiple_of(got, 8), h), t)
        cur = nxt
    for c in sends:
        c.wait_send()
    for c, l in tail:
        l.wait()
        c.wait()

def product_part(f_ref, q_ref, p_ref, F, Q, S, own, YR, XS, XR, P2, fsem, qs, qr, gs, gr, ys, yr, xs, xr, ps, pr):
    x, y, z, core = coords()
    row, col = lax.axis_index("row"), lax.axis_index("col")
    chunks, wide = Q.shape[0], Q.shape[3]
    half = chunks * wide
    sib = device(x, y, z, 1 - core)
    across = device((x + 2) % 4, y, z, core)
    beside = device(x + 1 - 2 * (x % 2), y, z, core)
    behind = device(3 - x, y, z, core)
    zs = [device(x, y, (z + k) % 4, core) for k in (1, 2, 3)]
    yy = [device(x, (y + k) % 4, z, core) for k in (1, 2, 3)]
    bar = pltpu.get_barrier_semaphore()
    for d in [sib, across, beside, behind] + zs + yy:
        pl.semaphore_signal(bar, inc=1, device_id=d, device_id_type=MESH)
    pl.semaphore_wait(bar, 10)
    lane = lambda first: pl.ds(pl.multiple_of(first, 128), wide)
    mine = pl.ds(pl.multiple_of(row * 128, 128), 128)
    acro = pl.ds(pl.multiple_of((row + 1 - 2 * (row % 2)) * 128, 128), 128)
    sends = []
    def go(c):
        c.start()
        sends.append(c)
        return c
    sq = [go(remote(q_ref.at[:, lane((1 - core) * half + ch * wide)], Q.at[ch, 1, mine, :], qs.at[ch], qr.at[ch], sib)) for ch in range(chunks)]
    fr = go(remote(f_ref, F.at[1], fsem.at[0], fsem.at[1], sib))
    fl = pltpu.make_async_copy(f_ref, F.at[0], fsem.at[2])
    fl.start()
    ql = [pltpu.make_async_copy(q_ref.at[:, lane(core * half + ch * wide)], Q.at[ch, 0, mine, :], qs.at[chunks + ch]) for ch in range(chunks)]
    for c in ql:
        c.start()
    def gat(ch, i, at, d):
        return go(remote(Q.at[ch, :, at, :], Q.at[ch, :, at, :], gs.at[ch, i], gr.at[ch, i], d))
    gx, gz = [], [[] for _ in range(chunks)]
    for ch in range(chunks):
        sq[ch].wait_recv()
        ql[ch].wait()
        gx.append(gat(ch, 0, mine, across))
    def near(ch):
        for k in range(3):
            gz[ch].append(gat(ch, 1 + k, mine, zs[k]))
    def forward(ch):
        gx[ch].wait_recv()
        for k in range(3):
            gz[ch].append(gat(ch, 4 + k, acro, zs[k]))
    near(0)
    forward(0)
    near(1)
    forward(1)
    ysend = [[] for _ in range(chunks)]
    xsend, psend = [None] * chunks, [None] * chunks
    xl = x % 2
    keep = pl.ds(pl.multiple_of(xl * 256, 256), 256)
    give = pl.ds(pl.multiple_of((1 - xl) * 256, 256), 256)
    def multiply(ch):
        for k in (2, 1, 3, 0):
            at = pl.ds(pl.multiple_of(((y + k) % 4) * 512, 512), 512)
            v = lax.dot_general(F[0, at, :], Q[ch, 0], NN, preferred_element_type=F32)
            v = v + lax.dot_general(F[1, at, :], Q[ch, 1], NN, preferred_element_type=F32)
            if k == 0:
                own[ch] = v
            else:
                S[ch, k - 1] = v.astype(BF)
                ysend[ch].append(go(remote(S.at[ch, k - 1], YR.at[ch, k - 1], ys.at[ch, k - 1], yr.at[ch, k - 1], yy[k - 1])))
    def add(ch):
        for c in ysend[ch]:
            c.wait_recv()
        def total(at):
            return own[ch, at, :] + ((YR[ch, 0, at, :].astype(F32) + YR[ch, 1, at, :].astype(F32)) + YR[ch, 2, at, :].astype(F32))
        XS[ch] = total(give).astype(BF)
        xsend[ch] = go(remote(XS.at[ch], XR.at[ch], xs.at[ch], xr.at[ch], beside))
        own[ch, keep, :] = total(keep)
    def finish(ch):
        xsend[ch].wait_recv()
        at = lane(core * half + ch * wide)
        P2[:, at] = (own[ch, keep, :] + XR[ch].astype(F32)).astype(BF)
        psend[ch] = go(remote(P2.at[:, at], P2.at[:, at], ps.at[ch], pr.at[ch], sib))
    for ch in range(chunks):
        if ch + 2 < chunks:
            near(ch + 2)
            forward(ch + 2)
        for c in gz[ch]:
            c.wait_recv()
        if ch == 0:
            fl.wait()
            fr.wait_recv()
        multiply(ch)
        if ch >= 2:
            add(ch - 2)
        if ch >= 3:
            finish(ch - 3)
    add(chunks - 2)
    finish(chunks - 3)
    add(chunks - 1)
    finish(chunks - 2)
    finish(chunks - 1)
    for c in psend:
        c.wait_recv()
    p_ref[...] = P2[...]
    for c in sends:
        c.wait_send()

def product_gram_kernel(f_ref, q_ref, g_ref, p_ref, *scratch):
    product_part(f_ref, q_ref, p_ref, *scratch[:19])
    gram_part(scratch[7], g_ref, *scratch[19:])


def product_gram(factor, slab, chunks=8):
    n = slab.shape[1]
    rows, cols = factor.shape
    wide = n // 2 // chunks
    _, starts = strips(n)
    tall = starts[-1] * 256 // 12
    dma = pltpu.SemaphoreType.DMA
    vm = pltpu.VMEM
    return pl.pallas_call(
        product_gram_kernel,
        out_shape=[jax.ShapeDtypeStruct((2, 6, tall, 128), F32), jax.ShapeDtypeStruct((256, n), BF)],
        in_specs=[pl.BlockSpec(memory_space=pl.ANY)] * 2,
        out_specs=[pl.BlockSpec(memory_space=pl.ANY), pl.BlockSpec(memory_space=pltpu.VMEM)],
        scratch_shapes=[
            vm((2, rows, cols), BF), vm((chunks, 2, cols, wide), BF), vm((chunks, 3, 512, wide), BF), vm((chunks, 512, wide), F32),
            vm((chunks, 3, 512, wide), BF), vm((chunks, 256, wide), BF), vm((chunks, 256, wide), BF), vm((256, n), BF),
            dma((3,)), dma((2 * chunks,)), dma((chunks,)), dma((chunks, 7)), dma((chunks, 7)), dma((chunks, 3)), dma((chunks, 3)),
            dma((chunks,)), dma((chunks,)), dma((chunks,)), dma((chunks,)),
        ] + [vm((6, tall, 128), F32)] * 3 + [vm((n, 256), BF)] + [dma((6, 6))] * 4 + [dma((3, 6))] * 3,
        compiler_params=pltpu.CompilerParams(collective_id=0, has_side_effects=True, vmem_limit_bytes=60 * 2**20),
        name="product_gram",
    )(factor, slab)


def split(x):
    hi = x.astype(BF)
    return hi, (x - hi.astype(F32)).astype(BF)


def factor_block(d_ref, w_ref, slot, width=16):
    n = 128
    rows_i = lax.broadcasted_iota(jnp.int32, (n, n), 0)
    cols_i = lax.broadcasted_iota(jnp.int32, (n, n), 1)
    w_ref[...] = jnp.where(rows_i == cols_i, 1.0, 0.0).astype(F32)
    np_ = n // width
    R, V = d_ref[:width, :], w_ref[:width, :]
    for p in range(np_):
        b0, m0, m1 = width * p, width * (p + 1), width * (p + 2)
        more = p < np_ - 1
        if more:
            N, NV = d_ref[m0:m1, :], w_ref[m0:m1, :]
            A = jnp.concatenate([R, N], 0)
            Z = jnp.concatenate([V, NV], 0)
        else:
            A, Z = R, V
        H = A.shape[0]
        fin = slot(p) if slot is not None else None
        C = [jnp.broadcast_to(A[:, b0 + b:b0 + b + 1], (H, n)) for b in range(width)]
        us, vs = [], []
        def sub(x, a):
            return x[a:a + 1, :]
        lo = 0
        for a in range(width):
            if a - lo == 8:
                C = [None if c is None else c[8:] for c in C]
                A, Z = A[8:], Z[8:]
                lo = a
            q = a - lo
            r = lax.rsqrt(sub(C[a], q))
            u, v = sub(A, q) * r, sub(Z, q) * r
            us.append(u); vs.append(v)
            ca = C[a] * r
            C[a] = None
            for b in range(a + 1, width):
                C[b] = C[b] - ca * jnp.broadcast_to(sub(ca, b - lo), ca.shape)
            A = A - ca * u
            Z = Z - ca * v
        U, W = jnp.concatenate(us, 0), jnp.concatenate(vs, 0)
        d_ref[b0:m0, :] = U
        w_ref[b0:m0, :] = W
        if more:
            R, V = A[width - lo:], Z[width - lo:]
        if fin is not None:
            fin()
        if p < np_ - 2:
            uh, ul = split(U)
            wh, wl = split(W)
            lhs = jnp.concatenate([uh, ul, uh], 0)
            rhs = jnp.concatenate([jnp.concatenate([uh, uh, ul], 0), jnp.concatenate([wh, wh, wl], 0)], 1)
            up = lax.dot_general(lhs, rhs, (((0,), (0,)), ((), ())), preferred_element_type=F32)
            d_ref[m1:, :] = d_ref[m1:, :] - up[m1:, :n]
            w_ref[m1:, :] = w_ref[m1:, :] - up[m1:, n:]
    d_ref[...] = jnp.where(rows_i <= cols_i, d_ref[...], 0.0)


B=256
NT=(((1,),(1,)),((),()))
NN=(((1,),(0,)),((),()))
def mm(a,b,dims): return lax.dot_general(a,b,dims,preferred_element_type=F32)
def mm3(ah,al,bh,bl,dims): return mm(ah,bh,dims)+(mm(ah,bl,dims)+mm(al,bh,dims))
def mm3f(a,b,dims):
    ah,al=split(a); bh,bl=split(b)
    return mm3(ah,al,bh,bl,dims)
def factor_solve_kernel(g_ref, p_ref, m_ref, x_ref, y_ref, A, Lh, Ll, mh, ml, ys, x_s, d_s, w_s, e_s, v_s, Wh, Wl, gsem, xs, xr):
    row, col = lax.axis_index("row"), lax.axis_index("col")
    core = col % 2
    i = 2 * (col // 2) + 1 - core
    to = (i % 8, 2 * row + i // 8)
    i = (col % 2) * 8 + row
    frm = (col // 2, (i // 2) * 2 + 1 - i % 2)
    bar = pltpu.get_barrier_semaphore()
    pl.semaphore_signal(bar, inc=1, device_id=frm, device_id_type=MESH)
    n = p_ref.shape[1]
    nb = n // B
    h = B // 2
    lens, starts = strips(n)
    copies = [
        pltpu.make_async_copy(
            g_ref.at[pl.ds(starts[c] * B, lens[c] * B), :],
            A.at[pl.ds((c // 2) * B, lens[c] * B), pl.ds(c * 128, 128)],
            gsem.at[c],
        )
        for c in range(len(lens))
    ]
    for c in copies: c.start()
    A[n:n+h, :] = p_ref[pl.ds(pl.multiple_of((1 - core) * h, h), h), :].astype(F32)
    A[n+h:, :] = jnp.zeros((A.shape[0]-n-h, n), F32)
    ys[...] = jnp.zeros_like(ys)
    Wh[...] = jnp.zeros_like(Wh); Wl[...] = jnp.zeros_like(Wl)
    mhi, mlo = split(m_ref[...])
    mh[...] = mhi; ml[...] = mlo
    bs = lambda i: pl.ds(pl.multiple_of(i*B, B), B)
    def step(k, carry, start=False, end=False):
        kp = jnp.maximum(k-1, 0)
        kn = jnp.minimum(k+1, nb-1)
        def put(ref, r, c, v): ref[r, c] = v
        def update(i, c, j):
            r, cc, jj = bs(i), bs(c), bs(j)
            v = A[r, cc] - mm3(Lh[r, jj], Ll[r, jj], Lh[cc, jj], Ll[cc, jj], NT)
            return lambda: put(A, r, cc, v)
        def panel(i, c):
            r, cc = bs(i), bs(c)
            ah, al = split(A[r, cc])
            hi, lo = split(mm3(ah, al, Wh[...], Wl[...], NT))
            def fin():
                Lh[r, cc] = hi; Ll[r, cc] = lo
            return fin
        def moment(i, c, dst):
            r, cc, dd = bs(i), bs(c), bs(dst)
            v = ys[:, dd] + mm3(mh[:, r], ml[:, r], Lh[r, cc], Ll[r, cc], NN)
            return lambda: put(ys, slice(None), dd, v)
        def slot(s):
            fins = []
            if s < 8:
                if s < (1 if end else nb-1):
                    i = k+1+s
                    fins.append(panel(jnp.where((k >= 1) & (i <= nb), i, 0), kp))
                if s >= 1 and (s == 1 or not end):
                    i = k+s
                    fins.append(update(jnp.where((k >= 1) & (i <= nb), i, 0), k, kp))
            else:
                for t in () if end else (2*(s-8), 2*(s-8)+1):
                    ok = (t < (nb-k)*k) & (k+1 < nb)
                    j = t // (nb-k)
                    i = k+1 + t - j*(nb-k)
                    fins.append(update(jnp.where(ok, i, 0), kn, jnp.where(ok, j, 0)))
                i = kp + (s-8)
                ok = (k >= 1) & (i < nb)
                if s < 10 or not end:
                    fins.append(moment(jnp.where(ok, i, 0), kp, jnp.where(ok, kp, nb)))
            def fin():
                for f in fins: f()
            return fin
        kk = pl.multiple_of(k*B, B)
        q0, q1 = pl.ds(kk, h), pl.ds(kk+h, h)
        nx = bs(k+1)
        d_s[...] = A[q0, q0]
        factor_block(d_s, w_s, None if start else slot)
        w0h, w0l = split(w_s[...])
        l00 = d_s[...].T
        a10h, a10l = split(A[q1, q0])
        l10h, l10l = split(mm3(a10h, a10l, w0h, w0l, NT))
        e_s[...] = A[q1, q1] - mm3(l10h, l10l, l10h, l10l, NT)
        nh, nl = split(A[nx, q0])
        n0h, n0l = split(mm3(nh, nl, w0h, w0l, NT))
        n1 = A[nx, q1] - mm3(n0h, n0l, l10h, l10l, NT)
        uh, ul = split(mm3(l10h, l10l, w0h, w0l, NN))
        factor_block(e_s, v_s, None if start else lambda s: slot(s+8))
        w1h, w1l = split(v_s[...])
        n1h, n1l = split(n1)
        n1h, n1l = split(mm3(n1h, n1l, w1h, w1l, NT))
        Lh[nx, q0] = n0h; Ll[nx, q0] = n0l
        Lh[nx, q1] = n1h; Ll[nx, q1] = n1l
        cn = bs(kn)
        A[nx, cn] = A[nx, cn] - (mm3(n0h, n0l, n0h, n0l, NT) + mm3(n1h, n1l, n1h, n1l, NT))
        w10h, w10l = split(-mm3(w1h, w1l, uh, ul, NN))
        z = jnp.zeros((h, h), BF)
        for W, a, b, c in ((Wh, w0h, w10h, w1h), (Wl, w0l, w10l, w1l)):
            W[:h, :h] = a; W[h:, :h] = b; W[h:, h:] = c
        l0, l1 = split(l00), split(e_s[...].T)
        for L, a, b, c in ((Lh, l0[0], l10h, l1[0]), (Ll, l0[1], l10l, l1[1])):
            L[q0, q0] = a; L[q0, q1] = z; L[q1, q0] = b; L[q1, q1] = c
        if not start:
            solved(kp)
        return carry
    def pass_on(c):
        at = bs(c)
        return remote(x_s.at[:, at], x_ref.at[:, at], xs.at[c], xr.at[c], to)
    def solved(c):
        at = bs(c)
        x_s[:, at] = (Lh[n:n+h, at].astype(F32) + Ll[n:n+h, at].astype(F32)).astype(BF)
        pass_on(c).start()
    for c in copies[:4]: c.wait()
    step(jnp.int32(0), 0, start=True)
    for c in copies[4:]: c.wait()
    pl.semaphore_wait(bar, 1)
    lax.fori_loop(1, nb - 1, step, 0)
    step(jnp.int32(nb - 1), 0, end=True)
    solved(nb - 1)
    last = slice(n-B, n)
    y_ref[:, :n-B] = ys[:, :n-B]
    y_ref[:, last] = mm3(mh[:, last], ml[:, last], Lh[last, last], Ll[last, last], NN)
    for c in range(nb): pass_on(c).wait()

def factor_solve(g, p, m):
    n = p.shape[1]
    vm = pltpu.VMEM
    return pl.pallas_call(factor_solve_kernel,
        out_shape=[jax.ShapeDtypeStruct((128,n),BF), jax.ShapeDtypeStruct((128,n),F32)],
        in_specs=[pl.BlockSpec(memory_space=pl.ANY), pl.BlockSpec(memory_space=pltpu.VMEM), pl.BlockSpec(memory_space=pltpu.VMEM)],
        out_specs=[pl.BlockSpec(memory_space=pl.ANY), pl.BlockSpec(memory_space=pltpu.VMEM)],
        scratch_shapes=[vm((n+B,n),F32),vm((n+B,n),BF),vm((n+B,n),BF),vm((128,n),BF),vm((128,n),BF),vm((128,n+B),F32),vm((128,n),BF),
          vm((128,128),F32),vm((128,128),F32),vm((128,128),F32),vm((128,128),F32),vm((B,B),BF),vm((B,B),BF),pltpu.SemaphoreType.DMA((n//128,)),pltpu.SemaphoreType.DMA((n//B,)),pltpu.SemaphoreType.DMA((n//B,))],
        compiler_params=pltpu.CompilerParams(collective_id=1, has_side_effects=True, vmem_limit_bytes=54*2**20),
        name="factor_solve")(g,p,m)


def body(factor, old_basis, first_moment):
    gram, rows = product_gram(factor, old_basis)
    new_basis, rotated_moment = factor_solve(gram.reshape(-1, 128), rows, first_moment)
    return (new_basis, rotated_moment)


def solution(mesh):
    placed = (P("row", "col"), P(("col", "row"), None), P(("col", "row"), None))
    return jax.shard_map(
        body,
        mesh=mesh,
        in_specs=placed,
        out_specs=(P(("col", "row"), None), P(("col", "row"), None)),
        check_vma=False,
    )
```
